32 devices in a mesh: replica: 16 (over z, y, x), tensor: 2 (over core).
Axes of the slice: x: 2, y: 2, z: 4, core: 2. Of those that a mesh axis runs over, the one named last changes fastest.
Arguments:
- requests: bfloat16 [12288, 8192], P('replica', 'tensor'), may hold values from -6 to 6
- value_weight: bfloat16 [8192, 1024], P('tensor'), may hold values from -0.0625 to 0.0625
- lowrank_shrink: bfloat16 [64, 64, 8192], P('replica', None, 'tensor'), may hold values from -0.0625 to 0.0625
- lowrank_expand: bfloat16 [64, 64, 1024], P('replica', None, 'tensor'), may hold values from -0.75 to 0.75
- slot_adapter_choice: int32 [16, 8], P('replica'), may hold values from 0 to 63, as said below
- request_row_slot: int32 [16, 768], P('replica'), may hold values from 0 to 7, never falling along the last dimension, each value on 1 to 192 neighbouring positions
Outputs:
- values_out: bfloat16 [12288, 1024], P('replica', 'tensor')
The draws below stay inside these ranges and needn't reach their ends.
Inputs may be any that keep to these rules, and one draw needn't show every extreme that they name: Slot s of replica p uses adapter slot_adapter_choice[p, s], stored on replica slot_adapter_choice[p, s] // 4; the 8 adapters of one replica are stored on 8 different replicas, and some replicas store an adapter of every replica. `request_row_slot`: A replica's rows are grouped by slot in increasing order; every slot has 1 to 192 rows, and some replica has a slot of exactly 192 rows.
All inputs are finite; a program needn't handle non-finite values.
Results may differ from the reference program's by a relative error of at most 0.0045.
Values may be sent and summed in bfloat16 or wider, within the bound.
No kernel may reach another device: no remote copies, remote signals or barrier semaphores. Data moves between devices by JAX's collectives and lax.ppermute only.
A program may use at most 128 MiB of HBM per device.

```python
import math
import jax
import jax.numpy as jnp
import numpy as np
from jax import lax

MODEL_WIDTH = 8192
VALUE_WIDTH = 1024
ADAPTER_RANK = 64
ROW_DEV = 768
ADP_DEV = 4
ROWS = 12288
ADAPTER_TOTAL = 64
SLOT_DEV = 8
SEG_MOST = 192
N_REPLICA = 16


def draw_slot_adapter_choice(key, part):
    keys = jax.random.split(jax.random.fold_in(key, 7), 3)
    ordering_list = jax.random.permutation(keys[0], N_REPLICA)
    popular_count = max(N_REPLICA // 16, 1)
    extra_credit = jnp.where(ordering_list < popular_count, 1 << 21, 0).astype(jnp.int32)
    random_jitter = jax.random.randint(keys[1], (N_REPLICA, N_REPLICA), 0, 1 << 20, dtype=jnp.int32)
    score_values = (random_jitter + extra_credit[None, :]) * N_REPLICA + jnp.arange(N_REPLICA, dtype=jnp.int32)[None, :]
    unused, homes = lax.top_k(score_values, SLOT_DEV)
    local_pick = jax.random.randint(keys[2], (N_REPLICA, SLOT_DEV), 0, ADP_DEV, dtype=jnp.int32)
    return (homes.astype(jnp.int32) * ADP_DEV + local_pick).astype(jnp.int32)


def shard_levels(rng, dims, cuts, low, high):
    loudness, own = 1.0, jax.random.fold_in(rng, 6)
    for position, blocks in cuts:
        draws = jnp.exp(jax.random.uniform(jax.random.fold_in(own, position), (blocks,), jnp.float32, low / len(cuts), high / len(cuts)))
        loudness = loudness * jnp.repeat(draws, dims[position] // blocks).reshape([-1 if axis == position else 1 for axis in range(len(dims))])
    return loudness


def profile(number_of, total, reach, skew):
    loads = [(1 << 20) // math.isqrt(standing ** skew) + 1 for standing in range(2, number_of + 1)]
    spare, given = total - reach - (number_of - 1), [1] * (number_of - 1)
    while spare > 0:
        free = [i for i in range(number_of - 1) if given[i] < reach]
        whole, budget = sum([loads[i] for i in free]), spare
        for i in free:
            extra = min(reach - given[i], max(1, budget * loads[i] // whole), spare)
            given[i] = given[i] + extra
            spare = spare - extra
    return np.array([reach] + given)


def uneven(key, number_of, total, most, slope):
    if number_of == 2:
        one = jax.random.randint(key, (), max(1, total - most), min(most, total - 1) + 1)
        return jnp.stack([one, total - one])
    sizes = jnp.asarray(profile(number_of, total, most, slope), jnp.int32)
    couples = (number_of - 1) // 2
    giver, taker = sizes[1:1 + 2 * couples:2], sizes[2:2 + 2 * couples:2]
    room = jnp.minimum(giver - 1, most - taker)
    shifted = jax.random.randint(jax.random.fold_in(key, 1), (couples,), 0, 1 << 20) % (room + 1)
    sizes = sizes.at[1:1 + 2 * couples:2].set(giver - shifted).at[2:2 + 2 * couples:2].set(taker + shifted)
    return sizes[jax.random.permutation(jax.random.fold_in(key, 2), number_of)]


def scatter_about(rng, dims, deviation, bound, cuts=(), kind=jnp.bfloat16):
    array = jax.random.normal(rng, dims, jnp.float32) * deviation
    if len(cuts) > 0:
        array = shard_levels(rng, dims, cuts, -0.22, 0.18) * array
    return jnp.clip(array, min=-bound, max=bound).astype(kind)


def setup_inputs(seed: int = 0) -> dict:
    key_list = jax.random.split(jax.random.key(seed), 7)
    requests = scatter_about(key_list[0], (ROWS, MODEL_WIDTH), 1.0, 6.0, ((0, 16), (1, 2)))
    value_weight = scatter_about(key_list[1], (MODEL_WIDTH, VALUE_WIDTH), MODEL_WIDTH ** -0.5, 0.0625, ((0, 2),))
    lowrank_shrink = scatter_about(key_list[2], (ADAPTER_TOTAL, ADAPTER_RANK, MODEL_WIDTH), MODEL_WIDTH ** -0.5, 0.0625, ((0, 16), (2, 2)))
    lowrank_expand = scatter_about(key_list[3], (ADAPTER_TOTAL, ADAPTER_RANK, VALUE_WIDTH), ADAPTER_RANK ** -0.5, 0.75, ((0, 16), (2, 2)))
    slot_adapter_choice = draw_slot_adapter_choice(jax.random.fold_in(key_list[6], 71), 0)
    request_row_slot = jax.vmap(lambda own: jnp.searchsorted(jnp.cumsum(uneven(own, SLOT_DEV, ROW_DEV, SEG_MOST, 2)), jnp.arange(ROW_DEV), side="right"))(jax.random.split(key_list[5], N_REPLICA)).reshape((N_REPLICA, ROW_DEV)).astype(jnp.int32)
    return {"requests": requests, "value_weight": value_weight, "lowrank_shrink": lowrank_shrink, "lowrank_expand": lowrank_expand, "slot_adapter_choice": slot_adapter_choice, "request_row_slot": request_row_slot}


lowrank_scale = 2.0


def reference(requests, value_weight, lowrank_shrink, lowrank_expand, slot_adapter_choice, request_row_slot):
    base_output = jnp.dot(requests, value_weight, preferred_element_type=jnp.float32)
    slot_range = jnp.arange(SLOT_DEV, dtype=jnp.int32)
    seg_range = jnp.arange(SEG_MOST, dtype=jnp.int32)
    row_range = jnp.arange(ROW_DEV, dtype=jnp.int32)

    def one_replica(replica_row):
        start_row = (replica_row * ROW_DEV).astype(jnp.int32)
        own_rows = lax.dynamic_slice_in_dim(requests, start_row, ROW_DEV, 0)
        row_slots = request_row_slot[replica_row]
        adapter_table = slot_adapter_choice[replica_row]
        shrink_blocks = jnp.take(lowrank_shrink, adapter_table, axis=0).astype(jnp.float32)
        expand_blocks = jnp.take(lowrank_expand, adapter_table, axis=0).astype(jnp.float32)
        onehot = (row_slots[:, None] == slot_range[None, :]).astype(jnp.int32)
        counts = jnp.sum(onehot, axis=0).astype(jnp.int32)
        starts = (jnp.cumsum(counts) - counts).astype(jnp.int32)
        row_index = jnp.clip(starts[:, None] + seg_range[None, :], 0, ROW_DEV - 1).astype(jnp.int32)
        valid_slot = seg_range[None, :] < counts[:, None]
        segments = jnp.take(own_rows, row_index, axis=0).astype(jnp.float32)
        segments = jnp.where(valid_slot[:, :, None], segments, jnp.float32(0.0))
        hidden = jnp.einsum("sjd,srd->sjr", segments, shrink_blocks).astype(jnp.bfloat16)
        adapter_out = jnp.einsum("sjr,sro->sjo", hidden.astype(jnp.float32), expand_blocks)
        offset = row_range - jnp.take(starts, row_slots, axis=0)
        flat_index = (row_slots * SEG_MOST + offset).astype(jnp.int32)
        return jnp.take(adapter_out.reshape(SLOT_DEV * SEG_MOST, VALUE_WIDTH), flat_index, axis=0)

    adapter_gathered = lax.map(one_replica, jnp.arange(N_REPLICA, dtype=jnp.int32)).reshape(ROWS, VALUE_WIDTH)
    return (base_output + lowrank_scale * adapter_gathered).astype(jnp.bfloat16)
```

```python
import functools

import jax
import jax.numpy as jnp
from jax import lax
from jax.experimental import pallas as pl
from jax.experimental.pallas import tpu as pltpu
from jax.sharding import PartitionSpec as P

lowrank_scale = 2.0
PLANE = 4
ROUND = 4
STATIC_ROUNDS = 6
LAG = 2 * ROUND


def plan_gathered(rows, size):
    own = lax.axis_index("replica")
    mine = jnp.arange(size, dtype=jnp.int32)[:, None] == own
    return lax.psum(jnp.where(mine, rows[None, :], 0), "replica")


def per_device_general(
    requests, value_weight, lowrank_shrink, lowrank_expand, slot_adapter_choice, request_row_slot, replicas
):
    rows_dev = requests.shape[0]
    holding_count = lowrank_shrink.shape[0]
    rank_extent = lowrank_shrink.shape[1]
    output_portion = lowrank_expand.shape[2]
    own_plan = slot_adapter_choice[0]
    row_slots = request_row_slot[0]
    slot_count = own_plan.shape[0]
    seg_most = max(2 * rows_dev // slot_count, 2)
    plan_every = plan_gathered(own_plan, replicas)
    own_index = lax.axis_index("replica")
    home_mine = own_plan // holding_count
    matched = plan_every // holding_count == own_index
    outbound_local = jnp.sum(jnp.where(matched, plan_every % holding_count, 0), axis=1)
    slot_range = jnp.arange(slot_count, dtype=jnp.int32)
    seg_range = jnp.arange(seg_most, dtype=jnp.int32)
    onehot = (row_slots[:, None] == slot_range[None, :]).astype(jnp.int32)
    counts = jnp.sum(onehot, axis=0)
    starts = jnp.cumsum(counts) - counts
    row_index = jnp.clip(starts[:, None] + seg_range[None, :], 0, rows_dev - 1)
    valid_slot = seg_range[None, :] < counts[:, None]
    segments = jnp.take(requests, row_index, axis=0)
    segments = jnp.where(valid_slot[:, :, None], segments, jnp.zeros((), jnp.bfloat16))
    base_term = jnp.dot(requests, value_weight, preferred_element_type=jnp.float32)
    base_output = lax.psum_scatter(base_term, "tensor", scatter_dimension=1, tiled=True)
    shrink_outbound = jnp.take(lowrank_shrink, outbound_local, axis=0)
    expand_outbound = jnp.take(lowrank_expand, outbound_local, axis=0)
    got_down = lax.all_to_all(shrink_outbound, "replica", split_axis=0, concat_axis=0, tiled=True)
    got_up = lax.all_to_all(expand_outbound, "replica", split_axis=0, concat_axis=0, tiled=True)
    shrink_blocks = jnp.take(got_down, home_mine, axis=0)
    expand_blocks = jnp.take(got_up, home_mine, axis=0)
    partial_value = jnp.einsum(
        "sjd,srd->sjr", segments, shrink_blocks, preferred_element_type=jnp.float32
    )
    summed = lax.psum(partial_value.reshape(slot_count, seg_most * rank_extent), "tensor")
    hidden = summed.reshape(slot_count, seg_most, rank_extent).astype(jnp.bfloat16)
    adapter_out = jnp.einsum(
        "sjr,sro->sjo", hidden, expand_blocks, preferred_element_type=jnp.float32
    )
    row_start = jnp.sum(onehot * starts[None, :], axis=1)
    offset = jnp.arange(rows_dev, dtype=jnp.int32) - row_start
    flat_index = row_slots * seg_most + offset
    adapter_row_block = jnp.take(
        adapter_out.reshape(slot_count * seg_most, output_portion), flat_index, axis=0
    )
    return (base_output + lowrank_scale * adapter_row_block).astype(jnp.bfloat16)


ANY = pl.BlockSpec(memory_space=pl.ANY)
SMEM = pl.BlockSpec(memory_space=pltpu.SMEM)


def copy_all(copies):
    for copy in copies:
        copy.start()
    for copy in copies:
        copy.wait()


def open_kernel(lanes, index_ref, *refs):
    parts, (store, *sends, sem) = refs[:PLANE], refs[PLANE:]
    holding = parts[0].shape[0]
    copy_all(
        [
            pltpu.make_async_copy(part, store.at[pl.ds(i * holding, holding)], sem.at[i])
            for i, part in enumerate(parts)
        ]
    )
    pick(lanes, index_ref, store, sends, 0, sem)


def pick(lanes, index_ref, store, sends, start, sem):
    copies = []
    for i, send in enumerate(sends):
        direction, first = i % 2, start + (i // 2) * ROUND
        for j in range(ROUND):
            source = index_ref[direction * lanes + first + j]
            copies.append(pltpu.make_async_copy(store.at[source], send.at[j], sem.at[len(copies)]))
    copy_all(copies)


def round_kernel(lanes, own_stripes, sending, step_ref, index_ref, up, down, store_in, store, *refs):
    *sends, sem = refs
    step = step_ref[0]
    copy_all(
        [
            pltpu.make_async_copy(
                got, store.at[pl.ds(own_stripes + i * lanes + step * ROUND, ROUND)], sem.at[i]
            )
            for i, got in enumerate((up, down))
        ]
    )
    if sending:
        pick(lanes, index_ref, store, sends, (step + 2) * ROUND, sem)


def pick_kernel(lanes, step_ref, index_ref, store, *refs):
    *sends, sem = refs
    pick(lanes, index_ref, store, sends, step_ref[0] * ROUND, sem)


def hidden_kernel(slots, rank, tile, width, k, index_ref, bound_ref, spot_ref, x_ref, *refs):
    weights, (out_ref, stacked) = refs[:slots], refs[slots:]
    step = pl.program_id(0)

    @pl.when(step == 0)
    def _():
        for s, w_ref in enumerate(weights):
            stacked[pl.ds(s * rank, rank), :] = w_ref[0, :, :width]
            out_ref[pl.ds(s * rank, rank), :] = w_ref[0, :, width:]

    products = lax.dot_general(
        stacked[...], x_ref[...], (((1,), (1,)), ((), ())), preferred_element_type=jnp.float32
    )
    row = step * tile + lax.broadcasted_iota(jnp.int32, (rank, tile), 1)
    total = jnp.zeros((rank, tile), jnp.float32)
    for s in range(slots):
        low, high = bound_ref[k * 2 * slots + s], bound_ref[k * 2 * slots + slots + s]
        chosen = (row >= low) & (row < high)
        total += jnp.where(chosen, products[s * rank : (s + 1) * rank, :], 0.0)
    for j in range(tile // 128):
        place = pl.multiple_of(slots * rank + (step * (tile // 128) + j) * rank, rank)
        out_ref[pl.ds(place, rank), :] = total[:, j * 128 : (j + 1) * 128].astype(out_ref.dtype)


def output_kernel(slots, rank, bound_ref, spot_ref, hidden_ref, base_ref, other_ref, *refs):
    stripes, (out_ref, expand, ) = refs[:PLANE], refs[PLANE:]
    step = pl.program_id(0)

    @pl.when(step == 0)
    def _():
        for k, stripe in enumerate(stripes):
            place = pl.multiple_of((spot_ref[0] ^ k) * 128, 128)
            expand[:, pl.ds(place, 128)] = stripe[...]

    row = step * 128 + lax.broadcasted_iota(jnp.int32, (rank, 128), 1)
    hidden = hidden_ref[...]
    pieces = []
    for s in range(slots):
        chosen = (row >= bound_ref[s]) & (row < bound_ref[slots + s])
        pieces.append(jnp.where(chosen, hidden, 0.0))
    spread = jnp.concatenate(pieces, axis=0).T.astype(jnp.bfloat16)
    adapter = jnp.dot(spread, expand[...], preferred_element_type=jnp.float32)
    total = base_ref[...] + other_ref[...].astype(jnp.float32) + lowrank_scale * adapter
    out_ref[...] = total.astype(out_ref.dtype)


def tables(plan, spot, layer, layers, group):
    adapters = jnp.arange(layers * group, dtype=jnp.int32)
    per_layer = plan.reshape(layers, -1)
    need = jnp.any(per_layer[:, :, None] == adapters, axis=1).reshape(layers, layers, group)
    need = jnp.stack([need, need[::-1, ::-1]])
    planes = jnp.arange(layers, dtype=jnp.int32)
    beyond = planes[:, None, None] > planes[None, :, None]
    reach = jnp.max(jnp.where(need & beyond, planes[:, None, None], planes[None, :, None]), axis=1)
    g = jnp.arange(group, dtype=jnp.int32)
    ahead = (reach[..., None, :] > reach[..., :, None]) | (
        (reach[..., None, :] == reach[..., :, None]) & (g[None, :] < g[:, None])
    )
    rank = jnp.sum(ahead.astype(jnp.int32), axis=-1)
    crossing = reach[:, None] > planes[None, :, None, None]
    crossing &= planes[None, None, :, None] <= planes[None, :, None, None]
    number = jnp.sum(crossing.astype(jnp.int32), axis=-1)
    first = {}
    total = jnp.zeros((2,), jnp.int32)
    for z in range(layers - 1):
        for s in range(z, -1, -1):
            if s == z:
                first[s, z] = jnp.zeros((2,), jnp.int32)
            else:
                first[s, z] = jnp.maximum(first[s + 1, z] + number[:, z, s + 1], first[s, z - 1] + LAG)
            total = jnp.maximum(total, first[s, z] + number[:, z, s])
    none = jnp.zeros((2,), jnp.int32)
    begin = jnp.stack(
        [jnp.stack([first.get((s, z), none) for s in range(layers)], 1) for z in range(layers)], 1
    )
    position = jnp.where(crossing, begin[..., None] + rank[:, None], -1)
    lanes = lanes_of(layers, group)
    level = jnp.stack([layer, layers - 1 - layer])
    sent = jnp.stack([position[d][level[d]] for d in range(2)])
    got = jnp.stack([position[d][jnp.maximum(level[d] - 1, 0)] for d in range(2)])
    home = (((g // (group // PLANE)) ^ spot) * (group // PLANE) + g % (group // PLANE))[None, None]
    area = group + jnp.arange(2, dtype=jnp.int32)[:, None, None] * lanes
    lies = jnp.where((planes == level[:, None])[..., None], home, area + got)
    at = jnp.arange(lanes, dtype=jnp.int32)
    hit = sent.reshape(2, 1, -1) == at[None, :, None]
    send_index = jnp.sum(jnp.where(hit, lies.reshape(2, 1, -1), 0), axis=-1)
    where = jnp.where((planes <= layer)[:, None], lies[0], lies[1][::-1]).reshape(-1)
    return send_index.reshape(-1), where, jnp.max(total)


def lanes_of(layers, group):
    most = layers * group // 2 + LAG
    return -(-most // ROUND) * ROUND


def per_device(
    requests, value_weight, lowrank_shrink, lowrank_expand, slot_adapter_choice, request_row_slot, replicas
):
    rows, features = requests.shape
    holding, rank, _ = lowrank_shrink.shape
    out_width = lowrank_expand.shape[2]
    slots = slot_adapter_choice.shape[1]
    layers = replicas // PLANE
    group = PLANE * holding
    width, ewidth = features // PLANE, out_width // PLANE
    lanes = lanes_of(layers, group)
    me = lax.axis_index("replica")
    layer, spot = me // PLANE, me % PLANE
    core = lax.axis_index("tensor")

    def swap(x, k):
        return lax.ppermute(x, "replica", [(i, i ^ k) for i in range(replicas)])

    def shift(x, by):
        return lax.ppermute(
            x, "replica", [(i, i + by) for i in range(replicas) if 0 <= i + by < replicas]
        )

    def stripe(k):
        c = spot ^ k
        return jnp.concatenate(
            [
                lax.dynamic_slice_in_dim(lowrank_shrink, c * width, width, 2),
                lax.dynamic_slice_in_dim(lowrank_expand, c * ewidth, ewidth, 2),
            ],
            axis=2,
        )

    parts = [stripe(0)] + [swap(stripe(k), k) for k in range(1, PLANE)]

    slot_range = jnp.arange(slots, dtype=jnp.int32)
    row_slots = request_row_slot[0]
    ends = jnp.sum((row_slots[:, None] <= slot_range[None, :]).astype(jnp.int32), axis=0)
    begins = jnp.sum((row_slots[:, None] < slot_range[None, :]).astype(jnp.int32), axis=0)
    own_row = jnp.concatenate([slot_adapter_choice[0], begins, ends])
    every = plan_gathered(own_row, replicas)
    plan = every[:, :slots]
    send_index, where, total = tables(plan, spot, layer, layers, group)
    plane_rows = jnp.stack(
        [lax.dynamic_index_in_dim(every, me ^ k, 0, keepdims=False) for k in range(PLANE)]
    )
    used = plane_rows[:, :slots].reshape(-1)
    adapters = jnp.arange(layers * group, dtype=jnp.int32)
    weight_index = jnp.sum(jnp.where(used[:, None] == adapters[None, :], where[None, :], 0), axis=1)
    bounds = plane_rows[:, slots:].reshape(-1)
    spot1 = spot.reshape(1)

    store_type = jax.ShapeDtypeStruct((group + 2 * lanes, rank, width + ewidth), jnp.bfloat16)
    send_type = jax.ShapeDtypeStruct((ROUND, rank, width + ewidth), jnp.bfloat16)
    rounds = min(STATIC_ROUNDS, lanes // ROUND)
    store, *sends = pl.pallas_call(
        functools.partial(open_kernel, lanes),
        out_shape=[store_type] + [send_type] * 4,
        in_specs=[SMEM] + [ANY] * PLANE,
        out_specs=[ANY] * 5,
        scratch_shapes=[pltpu.SemaphoreType.DMA((4 * ROUND,))],
        name="open_store",
    )(send_index, *parts)

    def keep(store, step, got, sending):
        result = pl.pallas_call(
            functools.partial(round_kernel, lanes, group, sending),
            out_shape=[store_type] + [send_type] * (2 * sending),
            in_specs=[SMEM, SMEM] + [ANY] * 3,
            out_specs=[ANY] * (1 + 2 * sending),
            scratch_shapes=[pltpu.SemaphoreType.DMA((2 * ROUND,))],
            input_output_aliases={4: 0},
            name="keep_round",
        )(step, send_index, *got, store)
        return result[0], result[1:]

    queue = [sends[:2], sends[2:]]
    flying = [(shift(up, PLANE), shift(down, -PLANE)) for up, down in queue]

    tied, _ = lax.optimization_barrier((requests, sends))
    x_parts = [swap(lax.dynamic_slice_in_dim(tied, (spot ^ k) * width, width, 1), k) for k in range(1, PLANE)]

    base = jnp.dot(requests, value_weight, preferred_element_type=jnp.float32)
    base_own = lax.dynamic_slice_in_dim(base, core * out_width, out_width, 1)
    base_away = lax.dynamic_slice_in_dim(base, (1 - core) * out_width, out_width, 1)
    base_other = lax.ppermute(base_away.astype(jnp.bfloat16), "tensor", [(0, 1), (1, 0)])

    for r in range(rounds):
        sending = r + 2 < rounds
        store, sends = keep(store, jnp.full((1,), r, jnp.int32), flying[r], sending)
        if sending:
            flying.append((shift(sends[0], PLANE), shift(sends[1], -PLANE)))

    def more(state):
        return state[0] * ROUND < total

    def extra(state):
        r, store = state
        step = r.reshape(1)
        up, down = pl.pallas_call(
            functools.partial(pick_kernel, lanes),
            out_shape=[send_type] * 2,
            in_specs=[SMEM, SMEM, ANY],
            out_specs=[ANY] * 2,
            scratch_shapes=[pltpu.SemaphoreType.DMA((2 * ROUND,))],
            name="pick_round",
        )(step, send_index, store)
        store, _ = keep(store, step, (shift(up, PLANE), shift(down, -PLANE)), False)
        return r + 1, store

    _, store = lax.while_loop(more, extra, (jnp.int32(rounds), store))

    tile = 256 if rows % 256 == 0 else 128
    height = slots * rank + rows // 128 * rank

    def partial_hidden(k, x):
        column = (lambda i, w, b, s: (i, s[0])) if k == 0 else (lambda i, w, b, s: (i, 0))
        return pl.pallas_call(
            functools.partial(hidden_kernel, slots, rank, tile, width, k),
            out_shape=jax.ShapeDtypeStruct((height, ewidth), jnp.bfloat16),
            grid_spec=pltpu.PrefetchScalarGridSpec(
                num_scalar_prefetch=3,
                grid=(rows // tile,),
                in_specs=[pl.BlockSpec((tile, width), column)]
                + [
                    pl.BlockSpec(
                        (1, rank, width + ewidth),
                        functools.partial(lambda j, i, w, b, s: (w[j], 0, 0), k * slots + s),
                    )
                    for s in range(slots)
                ],
                out_specs=pl.BlockSpec((height, ewidth), lambda i, w, b, s: (0, 0)),
                scratch_shapes=[pltpu.VMEM((slots * rank, width), jnp.bfloat16)],
            ),
            name="partial_hidden",
        )(weight_index, bounds, spot1, x, *([store] * slots))

    away = [swap(partial_hidden(k, x_parts[k - 1]), k) for k in range(1, PLANE)]
    blocks = [partial_hidden(0, requests)] + away
    split = slots * rank
    hidden_part = sum(b[split:].astype(jnp.float32) for b in blocks)
    hidden_other = lax.ppermute(hidden_part, "tensor", [(0, 1), (1, 0)])
    hidden = (hidden_part + hidden_other).astype(jnp.bfloat16).astype(jnp.float32)

    return pl.pallas_call(
        functools.partial(output_kernel, slots, rank),
        out_shape=jax.ShapeDtypeStruct((rows, out_width), jnp.bfloat16),
        grid_spec=pltpu.PrefetchScalarGridSpec(
            num_scalar_prefetch=2,
            grid=(rows // 128,),
            in_specs=[
                pl.BlockSpec((rank, 128), lambda i, b, s: (i, 0)),
                pl.BlockSpec((128, out_width), lambda i, b, s: (i, 0)),
                pl.BlockSpec((128, out_width), lambda i, b, s: (i, 0)),
            ]
            + [pl.BlockSpec((slots * rank, ewidth), lambda i, b, s: (0, 0))] * PLANE,
            out_specs=pl.BlockSpec((128, out_width), lambda i, b, s: (i, 0)),
            scratch_shapes=[pltpu.VMEM((slots * rank, out_width), jnp.bfloat16)],
        ),
        name="output",
    )(bounds[: 2 * slots], spot1, hidden, base_own, base_other, *blocks)


def solution(mesh):
    replicas = mesh.shape["replica"]
    striped = replicas == 16 and mesh.shape["tensor"] == 2
    return jax.shard_map(
        functools.partial(per_device if striped else per_device_general, replicas=replicas),
        mesh=mesh,
        in_specs=(
            P("replica", "tensor"),
            P("tensor", None),
            P("replica", None, "tensor"),
            P("replica", None, "tensor"),
            P("replica", None),
            P("replica", None),
        ),
        out_specs=P("replica", "tensor"),
        check_vma=False,
    )
```

```python
import functools

import jax
import jax.numpy as jnp
from jax import lax
from jax.experimental import pallas as pl
from jax.experimental.pallas import tpu as pltpu
from jax.sharding import PartitionSpec as P

lowrank_scale = 2.0
PLANE = 4
ROUND = 4
STATIC_ROUNDS = 6
LAG = 2 * ROUND


def plan_gathered(rows, size):
    own = lax.axis_index("replica")
    mine = jnp.arange(size, dtype=jnp.int32)[:, None] == own
    return lax.psum(jnp.where(mine, rows[None, :], 0), "replica")


def per_device_general(
    requests, value_weight, lowrank_shrink, lowrank_expand, slot_adapter_choice, request_row_slot, replicas
):
    rows_dev = requests.shape[0]
    holding_count = lowrank_shrink.shape[0]
    rank_extent = lowrank_shrink.shape[1]
    output_portion = lowrank_expand.shape[2]
    own_plan = slot_adapter_choice[0]
    row_slots = request_row_slot[0]
    slot_count = own_plan.shape[0]
    seg_most = max(2 * rows_dev // slot_count, 2)
    plan_every = plan_gathered(own_plan, replicas)
    own_index = lax.axis_index("replica")
    home_mine = own_plan // holding_count
    matched = plan_every // holding_count == own_index
    outbound_local = jnp.sum(jnp.where(matched, plan_every % holding_count, 0), axis=1)
    slot_range = jnp.arange(slot_count, dtype=jnp.int32)
    seg_range = jnp.arange(seg_most, dtype=jnp.int32)
    onehot = (row_slots[:, None] == slot_range[None, :]).astype(jnp.int32)
    counts = jnp.sum(onehot, axis=0)
    starts = jnp.cumsum(counts) - counts
    row_index = jnp.clip(starts[:, None] + seg_range[None, :], 0, rows_dev - 1)
    valid_slot = seg_range[None, :] < counts[:, None]
    segments = jnp.take(requests, row_index, axis=0)
    segments = jnp.where(valid_slot[:, :, None], segments, jnp.zeros((), jnp.bfloat16))
    base_term = jnp.dot(requests, value_weight, preferred_element_type=jnp.float32)
    base_output = lax.psum_scatter(base_term, "tensor", scatter_dimension=1, tiled=True)
    shrink_outbound = jnp.take(lowrank_shrink, outbound_local, axis=0)
    expand_outbound = jnp.take(lowrank_expand, outbound_local, axis=0)
    got_down = lax.all_to_all(shrink_outbound, "replica", split_axis=0, concat_axis=0, tiled=True)
    got_up = lax.all_to_all(expand_outbound, "replica", split_axis=0, concat_axis=0, tiled=True)
    shrink_blocks = jnp.take(got_down, home_mine, axis=0)
    expand_blocks = jnp.take(got_up, home_mine, axis=0)
    partial_value = jnp.einsum(
        "sjd,srd->sjr", segments, shrink_blocks, preferred_element_type=jnp.float32
    )
    summed = lax.psum(partial_value.reshape(slot_count, seg_most * rank_extent), "tensor")
    hidden = summed.reshape(slot_count, seg_most, rank_extent).astype(jnp.bfloat16)
    adapter_out = jnp.einsum(
        "sjr,sro->sjo", hidden, expand_blocks, preferred_element_type=jnp.float32
    )
    row_start = jnp.sum(onehot * starts[None, :], axis=1)
    offset = jnp.arange(rows_dev, dtype=jnp.int32) - row_start
    flat_index = row_slots * seg_most + offset
    adapter_row_block = jnp.take(
        adapter_out.reshape(slot_count * seg_most, output_portion), flat_index, axis=0
    )
    return (base_output + lowrank_scale * adapter_row_block).astype(jnp.bfloat16)


ANY = pl.BlockSpec(memory_space=pl.ANY)
HBM = pl.BlockSpec(memory_space=pltpu.HBM)
SMEM = pl.BlockSpec(memory_space=pltpu.SMEM)
VMEM = pl.BlockSpec(memory_space=pltpu.VMEM)
SHORT = pl.CostEstimate(flops=1, bytes_accessed=1, transcendentals=0)
AROUND = pl.CostEstimate(flops=1, bytes_accessed=50_000_000, transcendentals=0)


def grant(mebibytes):
    return pltpu.CompilerParams(vmem_limit_bytes=mebibytes * 1024 * 1024)


def copy_all(copies):
    for copy in copies:
        copy.start()
    for copy in copies:
        copy.wait()


def lanes_at(chip, width):
    return pl.ds(pl.multiple_of(chip * width, width), width)


def stripe_kernel(width, ewidth, me_ref, shrink, expand, placed, *refs):
    outs, sem = refs[:PLANE], refs[PLANE]
    spot = me_ref[0] % PLANE
    copies = []
    for k, out in enumerate(outs):
        chip = spot ^ k
        for source, n, start in ((shrink, width, 0), (expand, ewidth, width)):
            copies.append(
                pltpu.make_async_copy(
                    source.at[:, :, lanes_at(chip, n)], out.at[:, :, pl.ds(start, n)], sem.at[len(copies)]
                )
            )
    copy_all(copies)


def gate_kernel(*refs):
    pass


def gate(x, *after):
    return pl.pallas_call(
        gate_kernel,
        out_shape=jax.ShapeDtypeStruct(x.shape, x.dtype),
        in_specs=[ANY] * (1 + len(after)),
        out_specs=ANY,
        input_output_aliases={0: 0},
        compiler_params=grant(60),
        cost_estimate=SHORT,
        name="gate",
    )(x, *after)


def feature_kernel(width, x_ref, *refs):
    out, held, sem = refs[-3:]
    fetches = [
        pltpu.make_async_copy(x_ref.at[:, pl.ds(c * width, width)], held.at[c], sem.at[c]) for c in range(PLANE)
    ]
    puts = [pltpu.make_async_copy(held.at[c], out.at[c], sem.at[PLANE + c]) for c in range(PLANE)]
    for fetch in fetches:
        fetch.start()
    for fetch, put in zip(fetches, puts):
        fetch.wait()
        put.start()
    for put in puts:
        put.wait()


def open_kernel(holding, index_ref, *refs):
    parts, sends = refs[:PLANE], refs[-4:]
    for i, send in enumerate(sends):
        for j in range(ROUND):
            source = index_ref[i % 2, (i // 2) * ROUND + j]
            for k, part in enumerate(parts):

                @pl.when(source // holding == k)
                def _(part=part, send=send, j=j, source=source):
                    send[j] = part[source % holding]


def lay_kernel(holding, *refs):
    parts, (store, sem) = refs[:PLANE], refs[-2:]
    copy_all(
        [
            pltpu.make_async_copy(part.at[j], store.at[i * holding + j], sem.at[i * holding + j])
            for i, part in enumerate(parts)
            for j in range(holding)
        ]
    )


def pick(index_ref, store, sends, start, sem):
    copy_all(
        [
            pltpu.make_async_copy(store.at[index_ref[i, start + j]], send.at[j], sem.at[i * ROUND + j])
            for i, send in enumerate(sends)
            for j in range(ROUND)
        ]
    )


def round_kernel(lanes, own_stripes, sending, step_ref, index_ref, up, down, store_in, *refs):
    sends, sem = refs[len(refs) - 1 - 2 * sending : -1], refs[-1]
    store = refs[len(refs) - 2 - 2 * sending]
    step = step_ref[0]
    puts = [
        pltpu.make_async_copy(
            got.at[j], store.at[own_stripes + i * lanes + step * ROUND + j], sem.at[i * ROUND + j]
        )
        for i, got in enumerate((up, down))
        for j in range(ROUND)
    ]
    for put in puts:
        put.start()
    for i, send in enumerate(sends):
        came, area = (up, down)[i], own_stripes + i * lanes + step * ROUND
        for j in range(ROUND):
            source = index_ref[i, (step + 2) * ROUND + j]
            fresh = (source >= area) & (source < area + ROUND)
            fetch = pltpu.make_async_copy(
                store.at[source], send.at[j], sem.at[(2 + i) * ROUND + j]
            )

            @pl.when(fresh)
            def _(came=came, send=send, j=j, at=source - area):
                send[j] = came[jnp.clip(at, 0, ROUND - 1)]

            @pl.when(jnp.logical_not(fresh))
            def _(fetch=fetch):
                fetch.start()

    for i, send in enumerate(sends):
        area = own_stripes + i * lanes + step * ROUND
        for j in range(ROUND):
            source = index_ref[i, (step + 2) * ROUND + j]
            fetch = pltpu.make_async_copy(
                store.at[source], send.at[j], sem.at[(2 + i) * ROUND + j]
            )

            @pl.when((source < area) | (source >= area + ROUND))
            def _(fetch=fetch):
                fetch.wait()

    for put in puts:
        put.wait()


def pick_kernel(step_ref, index_ref, store, *refs):
    *sends, sem = refs
    pick(index_ref, store, sends, step_ref[0] * ROUND, sem)


def row_kernel(slots, replicas, me_ref, plan_ref, row_slot_ref, out_ref):
    row = lax.broadcasted_iota(jnp.int32, (replicas, 128), 0)
    lane = lax.broadcasted_iota(jnp.int32, (replicas, 128), 1)
    row_slots = row_slot_ref[...]
    total = jnp.zeros((replicas, 128), jnp.int32)
    begin = jnp.int32(0)
    for s in range(slots):
        end = jnp.sum((row_slots <= s).astype(jnp.int32))
        total = jnp.where(lane == s, plan_ref[0, s], total)
        total = jnp.where(lane == slots + s, begin, total)
        total = jnp.where(lane == 2 * slots + s, end, total)
        begin = end
    out_ref[...] = jnp.where(row == me_ref[0], total, 0)


def table_kernel(layers, group, lanes, slots, me_ref, every_ref, send_ref, lies_ref, total_ref):
    layer, spot = me_ref[0] // PLANE, me_ref[0] % PLANE
    holding = group // PLANE
    row = lax.broadcasted_iota(jnp.int32, (8, 128), 0)
    lane = lax.broadcasted_iota(jnp.int32, (8, 128), 1)
    plane, g = lane // group, lane % group
    ids = jnp.where(row == 0, lane, (layers - 1 - plane) * group + g)
    asked = []
    for z in range(layers):
        found = jnp.zeros((8, 128), jnp.int32)
        for r in range(PLANE):
            for s in range(slots):
                found = jnp.where(ids == every_ref[z * PLANE + r, s], 1, found)
        asked.append(found)
    reach = plane
    for z in range(1, layers):
        need = jnp.where(row == 0, asked[z], asked[layers - 1 - z])
        reach = jnp.where((need > 0) & (plane < z), z, reach)
    marks = [jnp.where((reach == z) & (plane < z), 1, 0) for z in range(1, layers)]
    stacked = jnp.concatenate([m.astype(jnp.float32) for m in marks], axis=0).astype(jnp.bfloat16)
    one = lax.broadcasted_iota(jnp.int32, (128, 128), 0)
    two = lax.broadcasted_iota(jnp.int32, (128, 128), 1)
    same = one // group == two // group
    before = jnp.where(same & (one < two), 1.0, 0.0).astype(jnp.bfloat16)
    same = jnp.where(same, 1.0, 0.0).astype(jnp.bfloat16)
    prior = jnp.dot(stacked, before, preferred_element_type=jnp.float32).astype(jnp.int32)
    count = jnp.dot(stacked, same, preferred_element_type=jnp.float32).astype(jnp.int32)
    rank = jnp.zeros((8, 128), jnp.int32)
    farther = jnp.zeros((8, 128), jnp.int32)
    number = [None] * (layers - 1)
    for z in range(layers - 2, -1, -1):
        rank += marks[z] * (prior[8 * z : 8 * z + 8] + farther)
        farther += count[8 * z : 8 * z + 8]
        number[z] = farther
    level = jnp.where(row == 0, layer, layers - 1 - layer)

    def after(x):
        return pltpu.roll(x, 128 - group, 1)

    far = jnp.maximum(number[2], LAG)
    far_0, own, both = after(far), after(number[1]), number[2]
    own_end = own + jnp.where(own > far_0, both, 0)
    rest = jnp.maximum(far_0 + both, own_end) - both
    on_second = jnp.where(
        plane == 0,
        rank + jnp.where(rank < both, far_0, rest),
        rank + jnp.where(rank >= far, pltpu.roll(number[2], group, 1), 0),
    )
    begin_1 = jnp.maximum(after(number[2]), LAG)
    begin_0 = jnp.maximum(after(begin_1 + number[2]), far_0 + LAG)
    on_third = rank + jnp.where(plane == 0, begin_0, jnp.where(plane == 1, begin_1, 0))
    places_on = [rank, on_second, on_third]
    total = jnp.zeros((8, 128), jnp.int32)
    sent = jnp.full((8, 128), -1, jnp.int32)
    got = jnp.zeros((8, 128), jnp.int32)
    for z in range(layers - 1):
        crosses = (reach > z) & (plane <= z)
        total = jnp.maximum(total, jnp.where(crosses, places_on[z] + 1, 0))
        sent = jnp.where((level == z) & crosses, places_on[z], sent)
        got = jnp.where((level - 1 == z) & crosses, places_on[z], got)
    home = ((g // holding) ^ spot) * holding + g % holding
    lies = jnp.where(plane == level, home, group + jnp.where(row == 0, 0, lanes) + got)
    lies_ref[...] = lies
    places = lies.astype(jnp.float32).astype(jnp.bfloat16)
    picked = []
    for d in range(2):
        hit = jnp.where(sent[d : d + 1, :] == one, 1.0, 0.0).astype(jnp.bfloat16)
        picked.append(
            lax.dot_general(places, hit, (((1,), (1,)), ((), ())), preferred_element_type=jnp.float32)
        )
    send_ref[...] = jnp.where(row == 0, picked[0], picked[1]).astype(jnp.int32)
    total_ref[0] = jnp.max(total)


def lane_bounds(slots, rank, every_ref, who):
    slot = lax.broadcasted_iota(jnp.int32, (1, slots * rank), 1) // rank
    low = jnp.zeros((1, slots * rank), jnp.int32)
    high = jnp.zeros((1, slots * rank), jnp.int32)
    for s in range(slots):
        low = jnp.where(slot == s, every_ref[who, slots + s], low)
        high = jnp.where(slot == s, every_ref[who, 2 * slots + s], high)
    return low, high


def hidden_kernel(slots, rank, half, width, k, me_ref, lies_ref, every_ref, first_ref, second_ref, *refs):
    weights, (out_ref, stacked) = refs[:slots], refs[slots:]
    for s, w_ref in enumerate(weights):
        stacked[pl.ds(s * rank, rank), :] = w_ref[0, :, :width]
        out_ref[pl.ds(s * rank, rank), :] = w_ref[0, :, width:]
    low, high = lane_bounds(slots, rank, every_ref, me_ref[0] ^ k)
    folded = []
    for i, x_ref in enumerate((first_ref, second_ref)):
        products = lax.dot_general(
            x_ref[...], stacked[...], (((1,), (1,)), ((), ())), preferred_element_type=jnp.float32
        )
        row = i * half + lax.broadcasted_iota(jnp.int32, (half, 1), 0)
        products = jnp.where((row >= low) & (row < high), products, 0.0)
        total = products[:, :128]
        for j in range(1, slots * rank // 128):
            total += products[:, j * 128 : (j + 1) * 128]
        folded.append(total + pltpu.roll(total, rank, 1))
    lane = lax.broadcasted_iota(jnp.int32, (half, 128), 1)
    out_ref[pl.ds(slots * rank, half), :] = jnp.where(lane < rank, folded[0], folded[1]).astype(out_ref.dtype)


def output_kernel(slots, rank, half, me_ref, every_ref, mine_ref, away_ref, base_ref, other_ref, *refs):
    stripes, (out_ref, expand) = refs[:PLANE], refs[PLANE:]
    step = pl.program_id(0)
    me = me_ref[0]

    @pl.when(step == 0)
    def _():
        for k, stripe in enumerate(stripes):
            place = pl.multiple_of(((me % PLANE) ^ k) * 128, 128)
            expand[:, pl.ds(place, 128)] = stripe[...]

    hidden = mine_ref[...] + away_ref[...]
    lane = lax.broadcasted_iota(jnp.int32, (half, 128), 1)
    hidden = jnp.where((lane >= rank) == (step == 1), hidden, pltpu.roll(hidden, rank, 1))
    low, high = lane_bounds(slots, rank, every_ref, me)
    row = step * half + lax.broadcasted_iota(jnp.int32, (half, 1), 0)
    spread = jnp.concatenate([hidden] * (slots * rank // 128), axis=1)
    spread = jnp.where((row >= low) & (row < high), spread, 0.0).astype(jnp.bfloat16)
    adapter = jnp.dot(spread, expand[...], preferred_element_type=jnp.float32)
    total = base_ref[...] + other_ref[...].astype(jnp.float32) + lowrank_scale * adapter
    out_ref[...] = total.astype(out_ref.dtype)


def base_kernel(out_width, core_ref, x_ref, w_ref, placed, placed_too, own_ref, away_ref, total_ref):
    step = pl.program_id(0)
    product = jnp.dot(x_ref[...], w_ref[...], preferred_element_type=jnp.float32)

    @pl.when(step == 0)
    def _():
        total_ref[...] = product

    @pl.when(step > 0)
    def _():
        total_ref[...] += product

    @pl.when(step == pl.num_programs(0) - 1)
    def _():
        own_ref[...] = total_ref[:, lanes_at(core_ref[0], out_width)]
        away_ref[...] = total_ref[:, lanes_at(1 - core_ref[0], out_width)].astype(away_ref.dtype)


def lanes_of(slots):
    return -(-(PLANE * slots + LAG) // ROUND) * ROUND


def per_device(
    requests, value_weight, lowrank_shrink, lowrank_expand, slot_adapter_choice, request_row_slot, replicas
):
    rows, features = requests.shape
    holding, rank, _ = lowrank_shrink.shape
    out_width = lowrank_expand.shape[2]
    slots = slot_adapter_choice.shape[1]
    layers = replicas // PLANE
    group = PLANE * holding
    width, ewidth = features // PLANE, out_width // PLANE
    lanes = lanes_of(slots)
    me = lax.axis_index("replica")
    layer, spot = me // PLANE, me % PLANE
    core = lax.axis_index("tensor")

    def swap(x, k):
        return lax.ppermute(x, "replica", [(i, i ^ k) for i in range(replicas)])

    def exchange(x):
        planes = [[p + i for i in range(PLANE)] for p in range(0, replicas, PLANE)]
        return lax.all_to_all(x, "replica", split_axis=0, concat_axis=0, tiled=True, axis_index_groups=planes)

    def shift(x, by):
        return lax.ppermute(
            x, "replica", [(i, i + by) for i in range(replicas) if 0 <= i + by < replicas]
        )

    me1 = me.reshape(1)
    every = pl.pallas_call(
        functools.partial(row_kernel, slots, replicas),
        out_shape=jax.ShapeDtypeStruct((replicas, 128), jnp.int32),
        in_specs=[SMEM, SMEM, VMEM],
        out_specs=VMEM,
        compiler_params=grant(2),
        cost_estimate=SHORT,
        name="plan_row",
    )(me1, slot_adapter_choice, request_row_slot)
    near = every = every + swap(every, 1) + swap(every, 2) + swap(every, 3)
    bit = PLANE
    while bit < replicas:
        every = every + swap(every, bit)
        bit *= 2
    send_index, lies, total = pl.pallas_call(
        functools.partial(table_kernel, layers, group, lanes, slots),
        out_shape=[
            jax.ShapeDtypeStruct((8, 128), jnp.int32),
            jax.ShapeDtypeStruct((8, 128), jnp.int32),
            jax.ShapeDtypeStruct((1,), jnp.int32),
        ],
        in_specs=[SMEM, SMEM],
        out_specs=[VMEM, VMEM, SMEM],
        compiler_params=grant(2),
        cost_estimate=SHORT,
        name="tables",
    )(me1, every)

    part_type = jax.ShapeDtypeStruct((holding, rank, width + ewidth), jnp.bfloat16)
    parts = pl.pallas_call(
        functools.partial(stripe_kernel, width, ewidth),
        out_shape=[part_type] * PLANE,
        in_specs=[SMEM, HBM, HBM, ANY],
        out_specs=[ANY] * PLANE,
        scratch_shapes=[pltpu.SemaphoreType.DMA((2 * PLANE,))],
        compiler_params=grant(1),
        cost_estimate=SHORT,
        name="stripes",
    )(me1, lowrank_shrink, lowrank_expand, near)
    parts = [parts[0]] + [swap(parts[k], k) for k in range(1, PLANE)]

    base_own, base_away = pl.pallas_call(
        functools.partial(base_kernel, out_width),
        out_shape=[
            jax.ShapeDtypeStruct((rows, out_width), jnp.float32),
            jax.ShapeDtypeStruct((rows, out_width), jnp.bfloat16),
        ],
        grid_spec=pltpu.PrefetchScalarGridSpec(
            num_scalar_prefetch=1,
            grid=(PLANE,),
            in_specs=[
                pl.BlockSpec((rows, width), lambda i, c: (0, i)),
                pl.BlockSpec((width, 2 * out_width), lambda i, c: (i, 0)),
                ANY,
                ANY,
            ],
            out_specs=[pl.BlockSpec((rows, out_width), lambda i, c: (0, 0))] * 2,
            scratch_shapes=[pltpu.VMEM((rows, 2 * out_width), jnp.float32)],
        ),
        compiler_params=grant(60),
        cost_estimate=pl.CostEstimate(
            flops=4 * rows * features * out_width, bytes_accessed=2 * features * (rows + 2 * out_width), transcendentals=0
        ),
        name="base",
    )(core.reshape(1), requests, value_weight, parts[0], lies)

    store_type = jax.ShapeDtypeStruct((group + 2 * lanes, rank, width + ewidth), jnp.bfloat16)
    send_type = jax.ShapeDtypeStruct((ROUND, rank, width + ewidth), jnp.bfloat16)
    rounds = min(STATIC_ROUNDS, lanes // ROUND)
    sends = pl.pallas_call(
        functools.partial(open_kernel, holding),
        out_shape=[send_type] * 4,
        in_specs=[SMEM] + [VMEM] * PLANE + [ANY],
        out_specs=[VMEM] * 4,
        compiler_params=grant(8),
        cost_estimate=SHORT,
        name="open_rounds",
    )(send_index, *parts, base_away)
    store = pl.pallas_call(
        functools.partial(lay_kernel, holding),
        out_shape=store_type,
        in_specs=[VMEM] * PLANE + [ANY],
        out_specs=ANY,
        scratch_shapes=[pltpu.SemaphoreType.DMA((group,))],
        compiler_params=grant(4),
        cost_estimate=SHORT,
        name="lay_store",
    )(*parts, sends[0])

    def keep(store, step, got, sending, late=()):
        result = pl.pallas_call(
            functools.partial(round_kernel, lanes, group, sending),
            out_shape=[store_type] + [send_type] * (2 * sending),
            in_specs=[SMEM, SMEM, VMEM, VMEM, ANY] + [ANY] * len(late),
            out_specs=[ANY] + [VMEM] * (2 * sending),
            scratch_shapes=[pltpu.SemaphoreType.DMA((4 * ROUND,))],
            input_output_aliases={4: 0},
            compiler_params=grant(6),
            cost_estimate=AROUND,
            name="keep_round",
        )(step, send_index, *got, store, *late)
        return result[0], result[1:]

    queue = [sends[:2], sends[2:]]
    flying = [(shift(up, PLANE), shift(down, -PLANE)) for up, down in queue]

    half = rows // 2
    after = (base_away,)
    x_parts = (
        pl.pallas_call(
            functools.partial(feature_kernel, width),
            out_shape=jax.ShapeDtypeStruct((PLANE, rows, width), jnp.bfloat16),
            in_specs=[HBM] + [ANY] * len(after),
            out_specs=ANY,
            scratch_shapes=[
                pltpu.VMEM((PLANE, rows, width), jnp.bfloat16),
                pltpu.SemaphoreType.DMA((2 * PLANE,)),
            ],
            compiler_params=grant(60),
            cost_estimate=SHORT,
            name="features",
        )(requests, *after)
    )
    x_all = exchange(gate(x_parts, lies, *parts[1:]))

    for r in range(rounds):
        sending = r + 2 < rounds
        if r == rounds - 1:
            base_other = lax.ppermute(gate(base_away, store), "tensor", [(0, 1), (1, 0)])
        store, sends = keep(store, jnp.full((1,), r, jnp.int32), flying[r], sending)
        if sending:
            flying.append((shift(sends[0], PLANE), shift(sends[1], -PLANE)))

    def more(state):
        return state[0] * ROUND < total[0]

    def extra(state):
        r, store = state
        step = r.reshape(1)
        up, down = pl.pallas_call(
            pick_kernel,
            out_shape=[send_type] * 2,
            in_specs=[SMEM, SMEM, ANY],
            out_specs=[VMEM] * 2,
            scratch_shapes=[pltpu.SemaphoreType.DMA((2 * ROUND,))],
            compiler_params=grant(4),
            cost_estimate=SHORT,
            name="pick_round",
        )(step, send_index, store)
        store, _ = keep(store, step, (shift(up, PLANE), shift(down, -PLANE)), False)
        return r + 1, store

    _, store = lax.while_loop(more, extra, (jnp.int32(rounds), store))

    split = slots * rank

    def partial_hidden(k):
        def piece_of(part, i, m, t, e):
            return (m[0] % PLANE) ^ k, part, 0

        def stripe_of(slot, i, m, t, e):
            adapter = e[m[0] ^ k, slot]
            plane = adapter // group
            from_below = t[0, adapter]
            from_above = t[1, (layers - 1 - plane) * group + adapter % group]
            return jnp.where(plane <= m[0] // PLANE, from_below, from_above), 0, 0

        return pl.pallas_call(
            functools.partial(hidden_kernel, slots, rank, half, width, k),
            out_shape=jax.ShapeDtypeStruct((split + half, ewidth), jnp.bfloat16),
            grid_spec=pltpu.PrefetchScalarGridSpec(
                num_scalar_prefetch=3,
                grid=(1,),
                in_specs=[
                    pl.BlockSpec((None, half, width), functools.partial(piece_of, part)) for part in range(2)
                ]
                + [
                    pl.BlockSpec((1, rank, width + ewidth), functools.partial(stripe_of, s))
                    for s in range(slots)
                ],
                out_specs=pl.BlockSpec((split + half, ewidth), lambda i, m, t, e: (0, 0)),
                scratch_shapes=[pltpu.VMEM((split, width), jnp.bfloat16)],
            ),
            compiler_params=grant(14),
            cost_estimate=SHORT,
            name="partial_hidden",
        )(me1, lies, every, x_all, x_all, *([store] * slots))

    away = [swap(partial_hidden(k), k) for k in range(1, PLANE)]
    blocks = [partial_hidden(0)] + away
    hidden_part = sum(b[split:].astype(jnp.float32) for b in blocks)
    hidden_other = lax.ppermute(hidden_part, "tensor", [(0, 1), (1, 0)])

    return pl.pallas_call(
        functools.partial(output_kernel, slots, rank, half),
        out_shape=jax.ShapeDtypeStruct((rows, out_width), jnp.bfloat16),
        grid_spec=pltpu.PrefetchScalarGridSpec(
            num_scalar_prefetch=2,
            grid=(2,),
            in_specs=[pl.BlockSpec((half, 128), lambda i, m, e: (0, 0))] * 2
            + [pl.BlockSpec((half, out_width), lambda i, m, e: (i, 0))] * 2
            + [pl.BlockSpec((split, ewidth), lambda i, m, e: (0, 0))] * PLANE,
            out_specs=pl.BlockSpec((half, out_width), lambda i, m, e: (i, 0)),
            scratch_shapes=[pltpu.VMEM((split, out_width), jnp.bfloat16)],
        ),
        compiler_params=grant(14),
        cost_estimate=SHORT,
        name="output",
    )(me1, every, hidden_part, hidden_other, base_own, base_other, *blocks)


def solution(mesh):
    replicas = mesh.shape["replica"]
    striped = replicas == 16 and mesh.shape["tensor"] == 2
    return jax.shard_map(
        functools.partial(per_device if striped else per_device_general, replicas=replicas),
        mesh=mesh,
        in_specs=(
            P("replica", "tensor"),
            P("tensor", None),
            P("replica", None, "tensor"),
            P("replica", None, "tensor"),
            P("replica", None),
            P("replica", None),
        ),
        out_specs=P("replica", "tensor"),
        check_vma=False,
    )
```

```python
import functools

import jax
import jax.numpy as jnp
from jax import lax
from jax.experimental import pallas as pl
from jax.experimental.pallas import tpu as pltpu
from jax.sharding import PartitionSpec as P

lowrank_scale = 2.0
PLANE = 4
ROUND = 4
STATIC_ROUNDS = 6
EXTRA = 2
LAG = 2 * ROUND


def plan_gathered(rows, size):
    own = lax.axis_index("replica")
    mine = jnp.arange(size, dtype=jnp.int32)[:, None] == own
    return lax.psum(jnp.where(mine, rows[None, :], 0), "replica")


def per_device_general(
    requests, value_weight, lowrank_shrink, lowrank_expand, slot_adapter_choice, request_row_slot, replicas
):
    rows_dev = requests.shape[0]
    holding_count = lowrank_shrink.shape[0]
    rank_extent = lowrank_shrink.shape[1]
    output_portion = lowrank_expand.shape[2]
    own_plan = slot_adapter_choice[0]
    row_slots = request_row_slot[0]
    slot_count = own_plan.shape[0]
    seg_most = max(2 * rows_dev // slot_count, 2)
    plan_every = plan_gathered(own_plan, replicas)
    own_index = lax.axis_index("replica")
    home_mine = own_plan // holding_count
    matched = plan_every // holding_count == own_index
    outbound_local = jnp.sum(jnp.where(matched, plan_every % holding_count, 0), axis=1)
    slot_range = jnp.arange(slot_count, dtype=jnp.int32)
    seg_range = jnp.arange(seg_most, dtype=jnp.int32)
    onehot = (row_slots[:, None] == slot_range[None, :]).astype(jnp.int32)
    counts = jnp.sum(onehot, axis=0)
    starts = jnp.cumsum(counts) - counts
    row_index = jnp.clip(starts[:, None] + seg_range[None, :], 0, rows_dev - 1)
    valid_slot = seg_range[None, :] < counts[:, None]
    segments = jnp.take(requests, row_index, axis=0)
    segments = jnp.where(valid_slot[:, :, None], segments, jnp.zeros((), jnp.bfloat16))
    base_term = jnp.dot(requests, value_weight, preferred_element_type=jnp.float32)
    base_output = lax.psum_scatter(base_term, "tensor", scatter_dimension=1, tiled=True)
    shrink_outbound = jnp.take(lowrank_shrink, outbound_local, axis=0)
    expand_outbound = jnp.take(lowrank_expand, outbound_local, axis=0)
    got_down = lax.all_to_all(shrink_outbound, "replica", split_axis=0, concat_axis=0, tiled=True)
    got_up = lax.all_to_all(expand_outbound, "replica", split_axis=0, concat_axis=0, tiled=True)
    shrink_blocks = jnp.take(got_down, home_mine, axis=0)
    expand_blocks = jnp.take(got_up, home_mine, axis=0)
    partial_value = jnp.einsum(
        "sjd,srd->sjr", segments, shrink_blocks, preferred_element_type=jnp.float32
    )
    summed = lax.psum(partial_value.reshape(slot_count, seg_most * rank_extent), "tensor")
    hidden = summed.reshape(slot_count, seg_most, rank_extent).astype(jnp.bfloat16)
    adapter_out = jnp.einsum(
        "sjr,sro->sjo", hidden, expand_blocks, preferred_element_type=jnp.float32
    )
    row_start = jnp.sum(onehot * starts[None, :], axis=1)
    offset = jnp.arange(rows_dev, dtype=jnp.int32) - row_start
    flat_index = row_slots * seg_most + offset
    adapter_row_block = jnp.take(
        adapter_out.reshape(slot_count * seg_most, output_portion), flat_index, axis=0
    )
    return (base_output + lowrank_scale * adapter_row_block).astype(jnp.bfloat16)


ANY = pl.BlockSpec(memory_space=pl.ANY)
HBM = pl.BlockSpec(memory_space=pltpu.HBM)
SMEM = pl.BlockSpec(memory_space=pltpu.SMEM)
VMEM = pl.BlockSpec(memory_space=pltpu.VMEM)
GATE = 60
SHORT = pl.CostEstimate(flops=1, bytes_accessed=1, transcendentals=0)
AROUND = pl.CostEstimate(flops=1, bytes_accessed=50_000_000, transcendentals=0)


def grant(mebibytes):
    return pltpu.CompilerParams(vmem_limit_bytes=mebibytes * 1024 * 1024)


def copy_all(copies):
    for copy in copies:
        copy.start()
    for copy in copies:
        copy.wait()


def lanes_at(chip, width):
    return pl.ds(pl.multiple_of(chip * width, width), width)


def stripe_kernel(width, ewidth, me_ref, shrink, expand, *refs):
    outs, sem = refs[:PLANE], refs[PLANE]
    spot = me_ref[0] % PLANE
    copies = []
    for k, out in enumerate(outs):
        chip = spot ^ k
        for source, n, start in ((shrink, width, 0), (expand, ewidth, width)):
            copies.append(
                pltpu.make_async_copy(
                    source.at[:, :, lanes_at(chip, n)], out.at[:, :, pl.ds(start, n)], sem.at[len(copies)]
                )
            )
    copy_all(copies)


def gate_kernel(*refs):
    pass


def gate(arrays, *after):
    n = len(arrays)
    return pl.pallas_call(
        gate_kernel,
        out_shape=[jax.ShapeDtypeStruct(x.shape, x.dtype) for x in arrays],
        in_specs=[ANY] * (n + len(after)),
        out_specs=[ANY] * n,
        input_output_aliases={i: i for i in range(n)},
        compiler_params=grant(GATE),
        cost_estimate=SHORT,
        name="gate",
    )(*arrays, *after)


def feature_kernel(width, x_ref, *refs):
    out, held, sem = refs[-3:]
    fetches = [
        pltpu.make_async_copy(x_ref.at[:, pl.ds(c * width, width)], held.at[c], sem.at[c]) for c in range(PLANE)
    ]
    puts = [pltpu.make_async_copy(held.at[c], out.at[c], sem.at[PLANE + c]) for c in range(PLANE)]
    for fetch in fetches:
        fetch.start()
    for fetch, put in zip(fetches, puts):
        fetch.wait()
        put.start()
    for put in puts:
        put.wait()


def open_kernel(holding, index_ref, *refs):
    parts, sends = refs[:PLANE], refs[-4:]
    for i, send in enumerate(sends):
        for j in range(ROUND):
            source = index_ref[i % 2, (i // 2) * ROUND + j]
            for k, part in enumerate(parts):

                @pl.when(source // holding == k)
                def _(part=part, send=send, j=j, source=source):
                    send[j] = part[source % holding]


def lay_kernel(holding, *refs):
    parts, (store, sem) = refs[:PLANE], refs[-2:]
    copy_all(
        [
            pltpu.make_async_copy(part.at[j], store.at[i * holding + j], sem.at[i * holding + j])
            for i, part in enumerate(parts)
            for j in range(holding)
        ]
    )


def round_kernel(lanes, own_stripes, sending, place_ref, index_ref, up, down, store_in, *refs):
    sends, sem = refs[len(refs) - 1 - 2 * sending : -1], refs[-1]
    store = refs[len(refs) - 2 - 2 * sending]
    count = up.shape[0]
    place = place_ref[0]
    puts = [
        pltpu.make_async_copy(
            got.at[j], store.at[own_stripes + i * lanes + place + j], sem.at[i * count + j]
        )
        for i, got in enumerate((up, down))
        for j in range(count)
    ]
    for put in puts:
        put.start()
    picks = []
    for i, send in enumerate(sends):
        came, area = (up, down)[i], own_stripes + i * lanes + place
        for j in range(count):
            source = index_ref[i, place + 2 * count + j]
            fresh = (source >= area) & (source < area + count)
            fetch = pltpu.make_async_copy(store.at[source], send.at[j], sem.at[(2 + i) * count + j])
            picks.append((fresh, fetch))

            @pl.when(fresh)
            def _(came=came, send=send, j=j, at=source - area):
                send[j] = came[jnp.clip(at, 0, count - 1)]

            @pl.when(jnp.logical_not(fresh))
            def _(fetch=fetch):
                fetch.start()

    for fresh, fetch in picks:

        @pl.when(jnp.logical_not(fresh))
        def _(fetch=fetch):
            fetch.wait()

    for put in puts:
        put.wait()


def pick_kernel(place_ref, index_ref, store, *refs):
    *sends, sem = refs
    copy_all(
        [
            pltpu.make_async_copy(
                store.at[index_ref[i, place_ref[0] + j]], send.at[j], sem.at[i * EXTRA + j]
            )
            for i, send in enumerate(sends)
            for j in range(EXTRA)
        ]
    )


def row_kernel(slots, replicas, me_ref, plan_ref, row_slot_ref, out_ref):
    row = lax.broadcasted_iota(jnp.int32, (replicas, 128), 0)
    lane = lax.broadcasted_iota(jnp.int32, (replicas, 128), 1)
    row_slots = row_slot_ref[...]
    total = jnp.zeros((replicas, 128), jnp.int32)
    begin = jnp.int32(0)
    for s in range(slots):
        end = jnp.sum((row_slots <= s).astype(jnp.int32))
        total = jnp.where(lane == s, plan_ref[0, s], total)
        total = jnp.where(lane == slots + s, begin, total)
        total = jnp.where(lane == 2 * slots + s, end, total)
        begin = end
    out_ref[...] = jnp.where(row == me_ref[0], total, 0)


def table_kernel(layers, group, lanes, slots, me_ref, every_ref, send_ref, lies_ref, total_ref):
    layer, spot = me_ref[0] // PLANE, me_ref[0] % PLANE
    holding = group // PLANE
    row = lax.broadcasted_iota(jnp.int32, (8, 128), 0)
    lane = lax.broadcasted_iota(jnp.int32, (8, 128), 1)
    plane, g = lane // group, lane % group
    ids = jnp.where(row == 0, lane, (layers - 1 - plane) * group + g)
    asked = []
    for z in range(layers):
        found = jnp.zeros((8, 128), jnp.int32)
        for r in range(PLANE):
            for s in range(slots):
                found = jnp.where(ids == every_ref[z * PLANE + r, s], 1, found)
        asked.append(found)
    reach = plane
    for z in range(1, layers):
        need = jnp.where(row == 0, asked[z], asked[layers - 1 - z])
        reach = jnp.where((need > 0) & (plane < z), z, reach)
    marks = [jnp.where((reach == z) & (plane < z), 1, 0) for z in range(1, layers)]
    stacked = jnp.concatenate([m.astype(jnp.float32) for m in marks], axis=0).astype(jnp.bfloat16)
    one = lax.broadcasted_iota(jnp.int32, (128, 128), 0)
    two = lax.broadcasted_iota(jnp.int32, (128, 128), 1)
    same = one // group == two // group
    before = jnp.where(same & (one < two), 1.0, 0.0).astype(jnp.bfloat16)
    same = jnp.where(same, 1.0, 0.0).astype(jnp.bfloat16)
    prior = jnp.dot(stacked, before, preferred_element_type=jnp.float32).astype(jnp.int32)
    count = jnp.dot(stacked, same, preferred_element_type=jnp.float32).astype(jnp.int32)
    rank = jnp.zeros((8, 128), jnp.int32)
    farther = jnp.zeros((8, 128), jnp.int32)
    number = [None] * (layers - 1)
    for z in range(layers - 2, -1, -1):
        rank += marks[z] * (prior[8 * z : 8 * z + 8] + farther)
        farther += count[8 * z : 8 * z + 8]
        number[z] = farther
    level = jnp.where(row == 0, layer, layers - 1 - layer)

    def after(x):
        return pltpu.roll(x, 128 - group, 1)

    far = jnp.maximum(number[2], LAG)
    far_0, own, both = after(far), after(number[1]), number[2]
    own_end = own + jnp.where(own > far_0, both, 0)
    rest = jnp.maximum(far_0 + both, own_end) - both
    on_second = jnp.where(
        plane == 0,
        rank + jnp.where(rank < both, far_0, rest),
        rank + jnp.where(rank >= far, pltpu.roll(number[2], group, 1), 0),
    )
    begin_1 = jnp.maximum(after(number[2]), LAG)
    begin_0 = jnp.maximum(after(begin_1 + number[2]), far_0 + LAG)
    on_third = rank + jnp.where(plane == 0, begin_0, jnp.where(plane == 1, begin_1, 0))
    places_on = [rank, on_second, on_third]
    total = jnp.zeros((8, 128), jnp.int32)
    sent = jnp.full((8, 128), -1, jnp.int32)
    got = jnp.zeros((8, 128), jnp.int32)
    for z in range(layers - 1):
        crosses = (reach > z) & (plane <= z)
        total = jnp.maximum(total, jnp.where(crosses, places_on[z] + 1, 0))
        sent = jnp.where((level == z) & crosses, places_on[z], sent)
        got = jnp.where((level - 1 == z) & crosses, places_on[z], got)
    home = ((g // holding) ^ spot) * holding + g % holding
    lies = jnp.where(plane == level, home, group + jnp.where(row == 0, 0, lanes) + got)
    lies_ref[...] = lies
    places = lies.astype(jnp.float32).astype(jnp.bfloat16)
    picked = []
    for d in range(2):
        hit = jnp.where(sent[d : d + 1, :] == one, 1.0, 0.0).astype(jnp.bfloat16)
        picked.append(
            lax.dot_general(places, hit, (((1,), (1,)), ((), ())), preferred_element_type=jnp.float32)
        )
    send_ref[...] = jnp.where(row == 0, picked[0], picked[1]).astype(jnp.int32)
    total_ref[0] = jnp.max(total)


def lane_bounds(slots, rank, every_ref, who):
    slot = lax.broadcasted_iota(jnp.int32, (1, slots * rank), 1) // rank
    low = jnp.zeros((1, slots * rank), jnp.int32)
    high = jnp.zeros((1, slots * rank), jnp.int32)
    for s in range(slots):
        low = jnp.where(slot == s, every_ref[who, slots + s], low)
        high = jnp.where(slot == s, every_ref[who, 2 * slots + s], high)
    return low, high


def hidden_kernel(slots, rank, half, width, k, me_ref, lies_ref, every_ref, x_ref, *refs):
    weights, (out_ref, stacked) = refs[:slots], refs[slots:]
    for s, w_ref in enumerate(weights):
        stacked[pl.ds(s * rank, rank), :] = w_ref[0, :, :width]
        out_ref[pl.ds(s * rank, rank), :] = w_ref[0, :, width:]
    low, high = lane_bounds(slots, rank, every_ref, me_ref[0] ^ k)
    products = lax.dot_general(
        x_ref[...], stacked[...], (((1,), (1,)), ((), ())), preferred_element_type=jnp.float32
    )
    row = lax.broadcasted_iota(jnp.int32, (2 * half, 1), 0)
    products = jnp.where((row >= low) & (row < high), products, 0.0)
    total = products[:, :128]
    for j in range(1, slots * rank // 128):
        total += products[:, j * 128 : (j + 1) * 128]
    total += pltpu.roll(total, rank, 1)
    lane = lax.broadcasted_iota(jnp.int32, (half, 128), 1)
    out_ref[pl.ds(slots * rank, half), :] = jnp.where(lane < rank, total[:half], total[half:]).astype(out_ref.dtype)


def output_kernel(slots, rank, tile, me_ref, every_ref, mine_ref, away_ref, base_ref, other_ref, *refs):
    stripes, (out_ref, expand) = refs[:PLANE], refs[PLANE:]
    step = pl.program_id(0)
    me = me_ref[0]

    @pl.when(step == 0)
    def _():
        for k, stripe in enumerate(stripes):
            place = pl.multiple_of(((me % PLANE) ^ k) * 128, 128)
            expand[:, pl.ds(place, 128)] = stripe[...]

    hidden = mine_ref[...] + away_ref[...]
    lane = lax.broadcasted_iota(jnp.int32, (tile, 128), 1)
    hidden = jnp.where((lane >= rank) == (step == 1), hidden, pltpu.roll(hidden, rank, 1))
    low, high = lane_bounds(slots, rank, every_ref, me)
    row = step * tile + lax.broadcasted_iota(jnp.int32, (tile, 1), 0)
    spread = jnp.concatenate([hidden] * (slots * rank // 128), axis=1)
    spread = jnp.where((row >= low) & (row < high), spread, 0.0).astype(jnp.bfloat16)
    adapter = jnp.dot(spread, expand[...], preferred_element_type=jnp.float32)
    total = base_ref[...] + other_ref[...].astype(jnp.float32) + lowrank_scale * adapter
    out_ref[...] = total.astype(out_ref.dtype)


def base_kernel(out_width, core_ref, x_ref, w_ref, placed, placed_too, own_ref, away_ref, total_ref):
    step = pl.program_id(0)
    product = jnp.dot(x_ref[...], w_ref[...], preferred_element_type=jnp.float32)

    @pl.when(step == 0)
    def _():
        total_ref[...] = product

    @pl.when(step > 0)
    def _():
        total_ref[...] += product

    @pl.when(step == pl.num_programs(0) - 1)
    def _():
        own_ref[...] = total_ref[:, lanes_at(core_ref[0], out_width)]
        away_ref[...] = total_ref[:, lanes_at(1 - core_ref[0], out_width)].astype(away_ref.dtype)


def lanes_of(slots):
    return -(-(PLANE * slots + LAG) // ROUND) * ROUND


def per_device(
    requests, value_weight, lowrank_shrink, lowrank_expand, slot_adapter_choice, request_row_slot, replicas
):
    rows, features = requests.shape
    holding, rank, _ = lowrank_shrink.shape
    out_width = lowrank_expand.shape[2]
    slots = slot_adapter_choice.shape[1]
    layers = replicas // PLANE
    group = PLANE * holding
    width, ewidth = features // PLANE, out_width // PLANE
    lanes = lanes_of(slots)
    me = lax.axis_index("replica")
    layer, spot = me // PLANE, me % PLANE
    core = lax.axis_index("tensor")

    def swap(x, k):
        return lax.ppermute(x, "replica", [(i, i ^ k) for i in range(replicas)])

    def exchange(x):
        planes = [[p + i for i in range(PLANE)] for p in range(0, replicas, PLANE)]
        return lax.all_to_all(x, "replica", split_axis=0, concat_axis=0, tiled=True, axis_index_groups=planes)

    def shift(x, by):
        return lax.ppermute(
            x, "replica", [(i, i + by) for i in range(replicas) if 0 <= i + by < replicas]
        )

    me1 = me.reshape(1)
    every = pl.pallas_call(
        functools.partial(row_kernel, slots, replicas),
        out_shape=jax.ShapeDtypeStruct((replicas, 128), jnp.int32),
        in_specs=[SMEM, SMEM, VMEM],
        out_specs=VMEM,
        compiler_params=grant(2),
        cost_estimate=SHORT,
        name="plan_row",
    )(me1, slot_adapter_choice, request_row_slot)
    near = every = every + swap(every, 1) + swap(every, 2) + swap(every, 3)
    bit = PLANE
    while bit < replicas:
        every = every + swap(every, bit)
        bit *= 2
    send_index, lies, total = pl.pallas_call(
        functools.partial(table_kernel, layers, group, lanes, slots),
        out_shape=[
            jax.ShapeDtypeStruct((8, 128), jnp.int32),
            jax.ShapeDtypeStruct((8, 128), jnp.int32),
            jax.ShapeDtypeStruct((1,), jnp.int32),
        ],
        in_specs=[SMEM, SMEM],
        out_specs=[VMEM, VMEM, SMEM],
        compiler_params=grant(2),
        cost_estimate=SHORT,
        name="tables",
    )(me1, every)

    part_type = jax.ShapeDtypeStruct((holding, rank, width + ewidth), jnp.bfloat16)
    parts = pl.pallas_call(
        functools.partial(stripe_kernel, width, ewidth),
        out_shape=[part_type] * PLANE,
        in_specs=[SMEM, ANY, ANY],
        out_specs=[VMEM] * PLANE,
        scratch_shapes=[pltpu.SemaphoreType.DMA((2 * PLANE,))],
        compiler_params=grant(60),
        cost_estimate=SHORT,
        name="stripes",
    )(me1, lowrank_shrink, lowrank_expand)
    own_part, *parts = gate(parts, near)
    parts = [own_part] + [swap(parts[k - 1], k) for k in range(1, PLANE)]

    base_own, base_away = pl.pallas_call(
        functools.partial(base_kernel, out_width),
        out_shape=[
            jax.ShapeDtypeStruct((rows, out_width), jnp.float32),
            jax.ShapeDtypeStruct((rows, out_width), jnp.bfloat16),
        ],
        grid_spec=pltpu.PrefetchScalarGridSpec(
            num_scalar_prefetch=1,
            grid=(PLANE,),
            in_specs=[
                pl.BlockSpec((rows, width), lambda i, c: (0, i)),
                pl.BlockSpec((width, 2 * out_width), lambda i, c: (i, 0)),
                ANY,
                ANY,
            ],
            out_specs=[pl.BlockSpec((rows, out_width), lambda i, c: (0, 0))] * 2,
            scratch_shapes=[pltpu.VMEM((rows, 2 * out_width), jnp.float32)],
        ),
        compiler_params=grant(60),
        cost_estimate=pl.CostEstimate(
            flops=4 * rows * features * out_width, bytes_accessed=2 * features * (rows + 2 * out_width), transcendentals=0
        ),
        name="base",
    )(core.reshape(1), requests, value_weight, parts[0], lies)

    store_type = jax.ShapeDtypeStruct((group + 2 * lanes, rank, width + ewidth), jnp.bfloat16)
    send_type = jax.ShapeDtypeStruct((ROUND, rank, width + ewidth), jnp.bfloat16)
    rounds = min(STATIC_ROUNDS, lanes // ROUND)
    sends = pl.pallas_call(
        functools.partial(open_kernel, holding),
        out_shape=[send_type] * 4,
        in_specs=[SMEM] + [VMEM] * PLANE + [ANY],
        out_specs=[VMEM] * 4,
        compiler_params=grant(8),
        cost_estimate=SHORT,
        name="open_rounds",
    )(send_index, *parts, base_away)
    store = pl.pallas_call(
        functools.partial(lay_kernel, holding),
        out_shape=store_type,
        in_specs=[VMEM] * PLANE + [ANY],
        out_specs=ANY,
        scratch_shapes=[pltpu.SemaphoreType.DMA((group,))],
        compiler_params=grant(4),
        cost_estimate=SHORT,
        name="lay_store",
    )(*parts, sends[0])

    def keep(store, step, got, sending, late=()):
        result = pl.pallas_call(
            functools.partial(round_kernel, lanes, group, sending),
            out_shape=[store_type] + [send_type] * (2 * sending),
            in_specs=[SMEM, SMEM, VMEM, VMEM, ANY] + [ANY] * len(late),
            out_specs=[ANY] + [VMEM] * (2 * sending),
            scratch_shapes=[pltpu.SemaphoreType.DMA((4 * ROUND,))],
            input_output_aliases={4: 0},
            compiler_params=grant(6),
            cost_estimate=AROUND,
            name="keep_round",
        )(step, send_index, *got, store, *late)
        return result[0], result[1:]

    queue = [sends[:2], sends[2:]]
    flying = [(shift(up, PLANE), shift(down, -PLANE)) for up, down in queue]

    half = rows // 2
    after = (base_away,)
    x_parts = (
        pl.pallas_call(
            functools.partial(feature_kernel, width),
            out_shape=jax.ShapeDtypeStruct((PLANE, rows, width), jnp.bfloat16),
            in_specs=[HBM] + [ANY] * len(after),
            out_specs=ANY,
            scratch_shapes=[
                pltpu.VMEM((PLANE, rows, width), jnp.bfloat16),
                pltpu.SemaphoreType.DMA((2 * PLANE,)),
            ],
            compiler_params=grant(60),
            cost_estimate=SHORT,
            name="features",
        )(requests, *after)
    )
    x_all = exchange(*gate([x_parts], sum(part[0, :8, :128] for part in parts[1:])))

    for r in range(rounds):
        sending = r + 2 < rounds
        if r == rounds - 1:
            base_other = lax.ppermute(gate([base_away], store)[0], "tensor", [(0, 1), (1, 0)])
        store, sends = keep(store, jnp.full((1,), r * ROUND, jnp.int32), flying[r], sending)
        if sending:
            flying.append((shift(sends[0], PLANE), shift(sends[1], -PLANE)))

    def more(state):
        return state[0] < total[0]

    def extra(state):
        place, store = state
        extra_type = jax.ShapeDtypeStruct((EXTRA, rank, width + ewidth), jnp.bfloat16)
        up, down = pl.pallas_call(
            pick_kernel,
            out_shape=[extra_type] * 2,
            in_specs=[SMEM, SMEM, ANY],
            out_specs=[VMEM] * 2,
            scratch_shapes=[pltpu.SemaphoreType.DMA((2 * EXTRA,))],
            compiler_params=grant(4),
            name="pick_round",
        )(place.reshape(1), send_index, store)
        store, _ = keep(store, place.reshape(1), (shift(up, PLANE), shift(down, -PLANE)), False)
        return place + EXTRA, store

    _, store = lax.while_loop(more, extra, (jnp.int32(rounds * ROUND), store))

    split = slots * rank

    def partial_hidden(k):
        def piece_of(i, m, t, e):
            return (m[0] % PLANE) ^ k, 0, 0

        def stripe_of(slot, i, m, t, e):
            adapter = e[m[0] ^ k, slot]
            plane = adapter // group
            from_below = t[0, adapter]
            from_above = t[1, (layers - 1 - plane) * group + adapter % group]
            return jnp.where(plane <= m[0] // PLANE, from_below, from_above), 0, 0

        return pl.pallas_call(
            functools.partial(hidden_kernel, slots, rank, half, width, k),
            out_shape=jax.ShapeDtypeStruct((split + half, ewidth), jnp.bfloat16),
            grid_spec=pltpu.PrefetchScalarGridSpec(
                num_scalar_prefetch=3,
                grid=(1,),
                in_specs=[pl.BlockSpec((None, rows, width), piece_of)]
                + [
                    pl.BlockSpec((1, rank, width + ewidth), functools.partial(stripe_of, s))
                    for s in range(slots)
                ],
                out_specs=pl.BlockSpec((split + half, ewidth), lambda i, m, t, e: (0, 0)),
                scratch_shapes=[pltpu.VMEM((split, width), jnp.bfloat16)],
            ),
            compiler_params=grant(16),
            cost_estimate=SHORT,
            name="partial_hidden",
        )(me1, lies, every, x_all, *([store] * slots))

    away = [swap(partial_hidden(k), k) for k in range(1, PLANE)]
    blocks = [partial_hidden(0)] + away
    hidden_part = sum(b[split:].astype(jnp.float32) for b in blocks)
    hidden_other = lax.ppermute(hidden_part, "tensor", [(0, 1), (1, 0)])

    return pl.pallas_call(
        functools.partial(output_kernel, slots, rank, half),
        out_shape=jax.ShapeDtypeStruct((rows, out_width), jnp.bfloat16),
        grid_spec=pltpu.PrefetchScalarGridSpec(
            num_scalar_prefetch=2,
            grid=(2,),
            in_specs=[pl.BlockSpec((half, 128), lambda i, m, e: (0, 0))] * 2
            + [pl.BlockSpec((half, out_width), lambda i, m, e: (i, 0))] * 2
            + [pl.BlockSpec((split, ewidth), lambda i, m, e: (0, 0))] * PLANE,
            out_specs=pl.BlockSpec((half, out_width), lambda i, m, e: (i, 0)),
            scratch_shapes=[pltpu.VMEM((split, out_width), jnp.bfloat16)],
        ),
        compiler_params=grant(14),
        cost_estimate=SHORT,
        name="output",
    )(me1, every, hidden_part, hidden_other, base_own, base_other, *blocks)


def solution(mesh):
    replicas = mesh.shape["replica"]
    striped = replicas == 16 and mesh.shape["tensor"] == 2
    return jax.shard_map(
        functools.partial(per_device if striped else per_device_general, replicas=replicas),
        mesh=mesh,
        in_specs=(
            P("replica", "tensor"),
            P("tensor", None),
            P("replica", None, "tensor"),
            P("replica", None, "tensor"),
            P("replica", None),
            P("replica", None),
        ),
        out_specs=P("replica", "tensor"),
        check_vma=False,
    )
```

```python
import functools

import jax
import jax.numpy as jnp
from jax import lax
from jax.experimental import pallas as pl
from jax.experimental.pallas import tpu as pltpu
from jax.sharding import PartitionSpec as P

lowrank_scale = 2.0
PLANE = 4
ROUND = 4
STATIC_ROUNDS = 6
EXTRA = 2
LAG = 2 * ROUND


def plan_gathered(rows, size):
    own = lax.axis_index("replica")
    mine = jnp.arange(size, dtype=jnp.int32)[:, None] == own
    return lax.psum(jnp.where(mine, rows[None, :], 0), "replica")


def per_device_general(
    requests, value_weight, lowrank_shrink, lowrank_expand, slot_adapter_choice, request_row_slot, replicas
):
    rows_dev = requests.shape[0]
    holding_count = lowrank_shrink.shape[0]
    rank_extent = lowrank_shrink.shape[1]
    output_portion = lowrank_expand.shape[2]
    own_plan = slot_adapter_choice[0]
    row_slots = request_row_slot[0]
    slot_count = own_plan.shape[0]
    seg_most = max(2 * rows_dev // slot_count, 2)
    plan_every = plan_gathered(own_plan, replicas)
    own_index = lax.axis_index("replica")
    home_mine = own_plan // holding_count
    matched = plan_every // holding_count == own_index
    outbound_local = jnp.sum(jnp.where(matched, plan_every % holding_count, 0), axis=1)
    slot_range = jnp.arange(slot_count, dtype=jnp.int32)
    seg_range = jnp.arange(seg_most, dtype=jnp.int32)
    onehot = (row_slots[:, None] == slot_range[None, :]).astype(jnp.int32)
    counts = jnp.sum(onehot, axis=0)
    starts = jnp.cumsum(counts) - counts
    row_index = jnp.clip(starts[:, None] + seg_range[None, :], 0, rows_dev - 1)
    valid_slot = seg_range[None, :] < counts[:, None]
    segments = jnp.take(requests, row_index, axis=0)
    segments = jnp.where(valid_slot[:, :, None], segments, jnp.zeros((), jnp.bfloat16))
    base_term = jnp.dot(requests, value_weight, preferred_element_type=jnp.float32)
    base_output = lax.psum_scatter(base_term, "tensor", scatter_dimension=1, tiled=True)
    shrink_outbound = jnp.take(lowrank_shrink, outbound_local, axis=0)
    expand_outbound = jnp.take(lowrank_expand, outbound_local, axis=0)
    got_down = lax.all_to_all(shrink_outbound, "replica", split_axis=0, concat_axis=0, tiled=True)
    got_up = lax.all_to_all(expand_outbound, "replica", split_axis=0, concat_axis=0, tiled=True)
    shrink_blocks = jnp.take(got_down, home_mine, axis=0)
    expand_blocks = jnp.take(got_up, home_mine, axis=0)
    partial_value = jnp.einsum(
        "sjd,srd->sjr", segments, shrink_blocks, preferred_element_type=jnp.float32
    )
    summed = lax.psum(partial_value.reshape(slot_count, seg_most * rank_extent), "tensor")
    hidden = summed.reshape(slot_count, seg_most, rank_extent).astype(jnp.bfloat16)
    adapter_out = jnp.einsum(
        "sjr,sro->sjo", hidden, expand_blocks, preferred_element_type=jnp.float32
    )
    row_start = jnp.sum(onehot * starts[None, :], axis=1)
    offset = jnp.arange(rows_dev, dtype=jnp.int32) - row_start
    flat_index = row_slots * seg_most + offset
    adapter_row_block = jnp.take(
        adapter_out.reshape(slot_count * seg_most, output_portion), flat_index, axis=0
    )
    return (base_output + lowrank_scale * adapter_row_block).astype(jnp.bfloat16)


ANY = pl.BlockSpec(memory_space=pl.ANY)
HBM = pl.BlockSpec(memory_space=pltpu.HBM)
SMEM = pl.BlockSpec(memory_space=pltpu.SMEM)
VMEM = pl.BlockSpec(memory_space=pltpu.VMEM)
GATE = 60
SHORT = pl.CostEstimate(flops=1, bytes_accessed=1, transcendentals=0)
AROUND = pl.CostEstimate(flops=1, bytes_accessed=50_000_000, transcendentals=0)


def grant(mebibytes):
    return pltpu.CompilerParams(vmem_limit_bytes=mebibytes * 1024 * 1024)


def copy_all(copies):
    for copy in copies:
        copy.start()
    for copy in copies:
        copy.wait()


def lanes_at(chip, width):
    return pl.ds(pl.multiple_of(chip * width, width), width)


def stripe_kernel(width, ewidth, me_ref, shrink, expand, *refs):
    outs, sem = refs[:PLANE], refs[PLANE]
    spot = me_ref[0] % PLANE
    copies = []
    for k, out in enumerate(outs):
        chip = spot ^ k
        for source, n, start in ((shrink, width, 0), (expand, ewidth, width)):
            copies.append(
                pltpu.make_async_copy(
                    source.at[:, :, lanes_at(chip, n)], out.at[:, :, pl.ds(start, n)], sem.at[len(copies)]
                )
            )
    copy_all(copies)


def gate_kernel(*refs):
    pass


def gate(arrays, *after):
    n = len(arrays)
    return pl.pallas_call(
        gate_kernel,
        out_shape=[jax.ShapeDtypeStruct(x.shape, x.dtype) for x in arrays],
        in_specs=[ANY] * (n + len(after)),
        out_specs=[ANY] * n,
        input_output_aliases={i: i for i in range(n)},
        compiler_params=grant(GATE),
        cost_estimate=SHORT,
        name="gate",
    )(*arrays, *after)


def open_kernel(holding, index_ref, *refs):
    parts, sends = refs[:PLANE], refs[-4:]
    for i, send in enumerate(sends):
        for j in range(ROUND):
            source = index_ref[i % 2, (i // 2) * ROUND + j]
            for k, part in enumerate(parts):

                @pl.when(source // holding == k)
                def _(part=part, send=send, j=j, source=source):
                    send[j] = part[source % holding]


def lay_kernel(holding, *refs):
    parts, (store, sem) = refs[:PLANE], refs[-2:]
    copy_all(
        [
            pltpu.make_async_copy(part.at[j], store.at[i * holding + j], sem.at[i * holding + j])
            for i, part in enumerate(parts)
            for j in range(holding)
        ]
    )


def round_kernel(lanes, own_stripes, sending, place_ref, index_ref, up, down, store_in, *refs):
    sends, sem = refs[len(refs) - 1 - 2 * sending : -1], refs[-1]
    store = refs[len(refs) - 2 - 2 * sending]
    count = up.shape[0]
    place = place_ref[0]
    puts = [
        pltpu.make_async_copy(
            got.at[j], store.at[own_stripes + i * lanes + place + j], sem.at[i * count + j]
        )
        for i, got in enumerate((up, down))
        for j in range(count)
    ]
    for put in puts:
        put.start()
    picks = []
    for i, send in enumerate(sends):
        came, area = (up, down)[i], own_stripes + i * lanes + place
        for j in range(count):
            source = index_ref[i, place + 2 * count + j]
            fresh = (source >= area) & (source < area + count)
            fetch = pltpu.make_async_copy(store.at[source], send.at[j], sem.at[(2 + i) * count + j])
            picks.append((fresh, fetch))

            @pl.when(fresh)
            def _(came=came, send=send, j=j, at=source - area):
                send[j] = came[jnp.clip(at, 0, count - 1)]

            @pl.when(jnp.logical_not(fresh))
            def _(fetch=fetch):
                fetch.start()

    for fresh, fetch in picks:

        @pl.when(jnp.logical_not(fresh))
        def _(fetch=fetch):
            fetch.wait()

    for put in puts:
        put.wait()


def pick_kernel(place_ref, index_ref, store, *refs):
    *sends, sem = refs
    copy_all(
        [
            pltpu.make_async_copy(
                store.at[index_ref[i, place_ref[0] + j]], send.at[j], sem.at[i * EXTRA + j]
            )
            for i, send in enumerate(sends)
            for j in range(EXTRA)
        ]
    )


def row_kernel(slots, replicas, me_ref, plan_ref, row_slot_ref, out_ref):
    row = lax.broadcasted_iota(jnp.int32, (replicas, 128), 0)
    lane = lax.broadcasted_iota(jnp.int32, (replicas, 128), 1)
    row_slots = row_slot_ref[...]
    total = jnp.zeros((replicas, 128), jnp.int32)
    begin = jnp.int32(0)
    for s in range(slots):
        end = jnp.sum((row_slots <= s).astype(jnp.int32))
        total = jnp.where(lane == s, plan_ref[0, s], total)
        total = jnp.where(lane == slots + s, begin, total)
        total = jnp.where(lane == 2 * slots + s, end, total)
        begin = end
    out_ref[...] = jnp.where(row == me_ref[0], total, 0)


def table_kernel(layers, group, lanes, slots, me_ref, every_ref, send_ref, lies_ref, total_ref):
    layer, spot = me_ref[0] // PLANE, me_ref[0] % PLANE
    holding = group // PLANE
    row = lax.broadcasted_iota(jnp.int32, (8, 128), 0)
    lane = lax.broadcasted_iota(jnp.int32, (8, 128), 1)
    plane, g = lane // group, lane % group
    ids = jnp.where(row == 0, lane, (layers - 1 - plane) * group + g)
    asked = []
    for z in range(layers):
        found = jnp.zeros((8, 128), jnp.int32)
        for r in range(PLANE):
            for s in range(slots):
                found = jnp.where(ids == every_ref[z * PLANE + r, s], 1, found)
        asked.append(found)
    reach = plane
    for z in range(1, layers):
        need = jnp.where(row == 0, asked[z], asked[layers - 1 - z])
        reach = jnp.where((need > 0) & (plane < z), z, reach)
    marks = [jnp.where((reach == z) & (plane < z), 1, 0) for z in range(1, layers)]
    stacked = jnp.concatenate([m.astype(jnp.float32) for m in marks], axis=0).astype(jnp.bfloat16)
    one = lax.broadcasted_iota(jnp.int32, (128, 128), 0)
    two = lax.broadcasted_iota(jnp.int32, (128, 128), 1)
    same = one // group == two // group
    before = jnp.where(same & (one < two), 1.0, 0.0).astype(jnp.bfloat16)
    same = jnp.where(same, 1.0, 0.0).astype(jnp.bfloat16)
    prior = jnp.dot(stacked, before, preferred_element_type=jnp.float32).astype(jnp.int32)
    count = jnp.dot(stacked, same, preferred_element_type=jnp.float32).astype(jnp.int32)
    rank = jnp.zeros((8, 128), jnp.int32)
    farther = jnp.zeros((8, 128), jnp.int32)
    number = [None] * (layers - 1)
    for z in range(layers - 2, -1, -1):
        rank += marks[z] * (prior[8 * z : 8 * z + 8] + farther)
        farther += count[8 * z : 8 * z + 8]
        number[z] = farther
    level = jnp.where(row == 0, layer, layers - 1 - layer)

    def after(x):
        return pltpu.roll(x, 128 - group, 1)

    far = jnp.maximum(number[2], LAG)
    far_0, own, both = after(far), after(number[1]), number[2]
    own_end = own + jnp.where(own > far_0, both, 0)
    rest = jnp.maximum(far_0 + both, own_end) - both
    on_second = jnp.where(
        plane == 0,
        rank + jnp.where(rank < both, far_0, rest),
        rank + jnp.where(rank >= far, pltpu.roll(number[2], group, 1), 0),
    )
    begin_1 = jnp.maximum(after(number[2]), LAG)
    begin_0 = jnp.maximum(after(begin_1 + number[2]), far_0 + LAG)
    on_third = rank + jnp.where(plane == 0, begin_0, jnp.where(plane == 1, begin_1, 0))
    places_on = [rank, on_second, on_third]
    total = jnp.zeros((8, 128), jnp.int32)
    sent = jnp.full((8, 128), -1, jnp.int32)
    got = jnp.zeros((8, 128), jnp.int32)
    for z in range(layers - 1):
        crosses = (reach > z) & (plane <= z)
        total = jnp.maximum(total, jnp.where(crosses, places_on[z] + 1, 0))
        sent = jnp.where((level == z) & crosses, places_on[z], sent)
        got = jnp.where((level - 1 == z) & crosses, places_on[z], got)
    home = ((g // holding) ^ spot) * holding + g % holding
    lies = jnp.where(plane == level, home, group + jnp.where(row == 0, 0, lanes) + got)
    lies_ref[...] = lies
    places = lies.astype(jnp.float32).astype(jnp.bfloat16)
    picked = []
    for d in range(2):
        hit = jnp.where(sent[d : d + 1, :] == one, 1.0, 0.0).astype(jnp.bfloat16)
        picked.append(
            lax.dot_general(places, hit, (((1,), (1,)), ((), ())), preferred_element_type=jnp.float32)
        )
    send_ref[...] = jnp.where(row == 0, picked[0], picked[1]).astype(jnp.int32)
    total_ref[0] = jnp.max(total)


def lane_bounds(slots, rank, every_ref, who):
    slot = lax.broadcasted_iota(jnp.int32, (1, slots * rank), 1) // rank
    low = jnp.zeros((1, slots * rank), jnp.int32)
    high = jnp.zeros((1, slots * rank), jnp.int32)
    for s in range(slots):
        low = jnp.where(slot == s, every_ref[who, slots + s], low)
        high = jnp.where(slot == s, every_ref[who, 2 * slots + s], high)
    return low, high


def hidden_kernel(slots, rank, half, width, k, me_ref, lies_ref, every_ref, x_ref, *refs):
    weights, (out_ref, stacked) = refs[:slots], refs[slots:]
    for s, w_ref in enumerate(weights):
        stacked[pl.ds(s * rank, rank), :] = w_ref[0, :, :width]
        out_ref[pl.ds(s * rank, rank), :] = w_ref[0, :, width:]
    low, high = lane_bounds(slots, rank, every_ref, me_ref[0] ^ k)
    products = lax.dot_general(
        x_ref[...], stacked[...], (((1,), (1,)), ((), ())), preferred_element_type=jnp.float32
    )
    row = lax.broadcasted_iota(jnp.int32, (2 * half, 1), 0)
    products = jnp.where((row >= low) & (row < high), products, 0.0)
    total = products[:, :128]
    for j in range(1, slots * rank // 128):
        total += products[:, j * 128 : (j + 1) * 128]
    total += pltpu.roll(total, rank, 1)
    lane = lax.broadcasted_iota(jnp.int32, (half, 128), 1)
    out_ref[pl.ds(slots * rank, half), :] = jnp.where(lane < rank, total[:half], total[half:]).astype(out_ref.dtype)


def output_kernel(slots, rank, tile, me_ref, every_ref, mine_ref, away_ref, base_ref, other_ref, *refs):
    stripes, (out_ref, expand) = refs[:PLANE], refs[PLANE:]
    step = pl.program_id(0)
    me = me_ref[0]

    @pl.when(step == 0)
    def _():
        for k, stripe in enumerate(stripes):
            place = pl.multiple_of(((me % PLANE) ^ k) * 128, 128)
            expand[:, pl.ds(place, 128)] = stripe[...]

    hidden = mine_ref[...] + away_ref[...]
    lane = lax.broadcasted_iota(jnp.int32, (tile, 128), 1)
    hidden = jnp.where((lane >= rank) == (step == 1), hidden, pltpu.roll(hidden, rank, 1))
    low, high = lane_bounds(slots, rank, every_ref, me)
    row = step * tile + lax.broadcasted_iota(jnp.int32, (tile, 1), 0)
    spread = jnp.concatenate([hidden] * (slots * rank // 128), axis=1)
    spread = jnp.where((row >= low) & (row < high), spread, 0.0).astype(jnp.bfloat16)
    adapter = jnp.dot(spread, expand[...], preferred_element_type=jnp.float32)
    total = base_ref[...] + other_ref[...].astype(jnp.float32) + lowrank_scale * adapter
    out_ref[...] = total.astype(out_ref.dtype)


def base_kernel(out_width, core_ref, x_ref, w_ref, placed, placed_too, own_ref, away_ref, parts_ref, total_ref):
    step = pl.program_id(0)
    parts_ref[0] = x_ref[...]

    @pl.when(step == 0)
    def _():
        total_ref[...] = jnp.dot(x_ref[...], w_ref[...], preferred_element_type=jnp.float32)

    @pl.when(step > 0)
    def _():
        total_ref[...] += jnp.dot(x_ref[...], w_ref[...], preferred_element_type=jnp.float32)

    @pl.when(step == pl.num_programs(0) - 1)
    def _():
        own_ref[...] = total_ref[:, lanes_at(core_ref[0], out_width)]
        away_ref[...] = total_ref[:, lanes_at(1 - core_ref[0], out_width)].astype(away_ref.dtype)


def lanes_of(slots):
    return -(-(PLANE * slots + LAG) // ROUND) * ROUND


def per_device(
    requests, value_weight, lowrank_shrink, lowrank_expand, slot_adapter_choice, request_row_slot, replicas
):
    rows, features = requests.shape
    holding, rank, _ = lowrank_shrink.shape
    out_width = lowrank_expand.shape[2]
    slots = slot_adapter_choice.shape[1]
    layers = replicas // PLANE
    group = PLANE * holding
    width, ewidth = features // PLANE, out_width // PLANE
    lanes = lanes_of(slots)
    me = lax.axis_index("replica")
    layer, spot = me // PLANE, me % PLANE
    core = lax.axis_index("tensor")

    def swap(x, k):
        return lax.ppermute(x, "replica", [(i, i ^ k) for i in range(replicas)])

    def exchange(x):
        planes = [[p + i for i in range(PLANE)] for p in range(0, replicas, PLANE)]
        return lax.all_to_all(x, "replica", split_axis=0, concat_axis=0, tiled=True, axis_index_groups=planes)

    def shift(x, by):
        return lax.ppermute(
            x, "replica", [(i, i + by) for i in range(replicas) if 0 <= i + by < replicas]
        )

    me1 = me.reshape(1)
    every = pl.pallas_call(
        functools.partial(row_kernel, slots, replicas),
        out_shape=jax.ShapeDtypeStruct((replicas, 128), jnp.int32),
        in_specs=[SMEM, SMEM, VMEM],
        out_specs=VMEM,
        compiler_params=grant(2),
        cost_estimate=SHORT,
        name="plan_row",
    )(me1, slot_adapter_choice, request_row_slot)
    near = every = every + swap(every, 1) + swap(every, 2) + swap(every, 3)
    part_type = jax.ShapeDtypeStruct((holding, rank, width + ewidth), jnp.bfloat16)
    parts = pl.pallas_call(
        functools.partial(stripe_kernel, width, ewidth),
        out_shape=[part_type] * PLANE,
        in_specs=[SMEM, ANY, ANY],
        out_specs=[VMEM] * PLANE,
        scratch_shapes=[pltpu.SemaphoreType.DMA((2 * PLANE,))],
        compiler_params=grant(60),
        cost_estimate=SHORT,
        name="stripes",
    )(me1, lowrank_shrink, lowrank_expand)
    own_part, *parts = gate(parts, near)
    parts = [own_part] + [swap(parts[k - 1], k) for k in range(1, PLANE)]

    base_own, base_away, x_parts = pl.pallas_call(
        functools.partial(base_kernel, out_width),
        out_shape=[
            jax.ShapeDtypeStruct((rows, out_width), jnp.float32),
            jax.ShapeDtypeStruct((rows, out_width), jnp.bfloat16),
            jax.ShapeDtypeStruct((PLANE, rows, width), jnp.bfloat16),
        ],
        grid_spec=pltpu.PrefetchScalarGridSpec(
            num_scalar_prefetch=1,
            grid=(PLANE,),
            in_specs=[
                pl.BlockSpec((rows, width), lambda i, c: (0, i)),
                pl.BlockSpec((width, 2 * out_width), lambda i, c: (i, 0)),
                ANY,
                ANY,
            ],
            out_specs=[pl.BlockSpec((rows, out_width), lambda i, c: (0, 0))] * 2
            + [pl.BlockSpec((1, rows, width), lambda i, c: (i, 0, 0))],
            scratch_shapes=[pltpu.VMEM((rows, 2 * out_width), jnp.float32)],
        ),
        compiler_params=grant(60),
        cost_estimate=pl.CostEstimate(
            flops=4 * rows * features * out_width, bytes_accessed=2 * features * (rows + 2 * out_width), transcendentals=0
        ),
        name="base",
    )(core.reshape(1), requests, value_weight, parts[0], near)

    every = gate([near], base_away)[0]
    bit = PLANE
    while bit < replicas:
        every = every + swap(every, bit)
        bit *= 2
    send_index, lies, total = pl.pallas_call(
        functools.partial(table_kernel, layers, group, lanes, slots),
        out_shape=[
            jax.ShapeDtypeStruct((8, 128), jnp.int32),
            jax.ShapeDtypeStruct((8, 128), jnp.int32),
            jax.ShapeDtypeStruct((1,), jnp.int32),
        ],
        in_specs=[SMEM, SMEM],
        out_specs=[VMEM, VMEM, SMEM],
        compiler_params=grant(2),
        cost_estimate=SHORT,
        name="tables",
    )(me1, every)


    store_type = jax.ShapeDtypeStruct((group + 2 * lanes, rank, width + ewidth), jnp.bfloat16)
    send_type = jax.ShapeDtypeStruct((ROUND, rank, width + ewidth), jnp.bfloat16)
    rounds = min(STATIC_ROUNDS, lanes // ROUND)
    sends = pl.pallas_call(
        functools.partial(open_kernel, holding),
        out_shape=[send_type] * 4,
        in_specs=[SMEM] + [VMEM] * PLANE + [ANY],
        out_specs=[VMEM] * 4,
        compiler_params=grant(8),
        cost_estimate=SHORT,
        name="open_rounds",
    )(send_index, *parts, base_away)
    store = pl.pallas_call(
        functools.partial(lay_kernel, holding),
        out_shape=store_type,
        in_specs=[VMEM] * PLANE + [ANY],
        out_specs=ANY,
        scratch_shapes=[pltpu.SemaphoreType.DMA((group,))],
        compiler_params=grant(4),
        cost_estimate=SHORT,
        name="lay_store",
    )(*parts, sends[0])

    def keep(store, step, got, sending, late=()):
        result = pl.pallas_call(
            functools.partial(round_kernel, lanes, group, sending),
            out_shape=[store_type] + [send_type] * (2 * sending),
            in_specs=[SMEM, SMEM, VMEM, VMEM, ANY] + [ANY] * len(late),
            out_specs=[ANY] + [VMEM] * (2 * sending),
            scratch_shapes=[pltpu.SemaphoreType.DMA((4 * ROUND,))],
            input_output_aliases={4: 0},
            compiler_params=grant(6),
            cost_estimate=AROUND,
            name="keep_round",
        )(step, send_index, *got, store, *late)
        return result[0], result[1:]

    queue = [sends[:2], sends[2:]]
    flying = [(shift(up, PLANE), shift(down, -PLANE)) for up, down in queue]

    half = rows // 2
    x_all = exchange(*gate([x_parts], sum(part[0, :8, :128] for part in parts[1:]), lies))

    for r in range(rounds):
        sending = r + 2 < rounds
        if r == rounds - 1:
            base_other = lax.ppermute(gate([base_away], store)[0], "tensor", [(0, 1), (1, 0)])
        store, sends = keep(store, jnp.full((1,), r * ROUND, jnp.int32), flying[r], sending)
        if sending:
            flying.append((shift(sends[0], PLANE), shift(sends[1], -PLANE)))

    def more(state):
        return state[0] < total[0]

    def extra(state):
        place, store = state
        extra_type = jax.ShapeDtypeStruct((EXTRA, rank, width + ewidth), jnp.bfloat16)
        up, down = pl.pallas_call(
            pick_kernel,
            out_shape=[extra_type] * 2,
            in_specs=[SMEM, SMEM, ANY],
            out_specs=[VMEM] * 2,
            scratch_shapes=[pltpu.SemaphoreType.DMA((2 * EXTRA,))],
            compiler_params=grant(4),
            name="pick_round",
        )(place.reshape(1), send_index, store)
        store, _ = keep(store, place.reshape(1), (shift(up, PLANE), shift(down, -PLANE)), False)
        return place + EXTRA, store

    _, store = lax.while_loop(more, extra, (jnp.int32(rounds * ROUND), store))

    split = slots * rank

    def partial_hidden(k):
        def piece_of(i, m, t, e):
            return (m[0] % PLANE) ^ k, 0, 0

        def stripe_of(slot, i, m, t, e):
            adapter = e[m[0] ^ k, slot]
            plane = adapter // group
            from_below = t[0, adapter]
            from_above = t[1, (layers - 1 - plane) * group + adapter % group]
            return jnp.where(plane <= m[0] // PLANE, from_below, from_above), 0, 0

        return pl.pallas_call(
            functools.partial(hidden_kernel, slots, rank, half, width, k),
            out_shape=jax.ShapeDtypeStruct((split + half, ewidth), jnp.bfloat16),
            grid_spec=pltpu.PrefetchScalarGridSpec(
                num_scalar_prefetch=3,
                grid=(1,),
                in_specs=[pl.BlockSpec((None, rows, width), piece_of)]
                + [
                    pl.BlockSpec((1, rank, width + ewidth), functools.partial(stripe_of, s))
                    for s in range(slots)
                ],
                out_specs=pl.BlockSpec((split + half, ewidth), lambda i, m, t, e: (0, 0)),
                scratch_shapes=[pltpu.VMEM((split, width), jnp.bfloat16)],
            ),
            compiler_params=grant(16),
            cost_estimate=SHORT,
            name="partial_hidden",
        )(me1, lies, every, x_all, *([store] * slots))

    away = [swap(partial_hidden(k), k) for k in range(1, PLANE)]
    blocks = [partial_hidden(0)] + away
    hidden_part = sum(b[split:].astype(jnp.float32) for b in blocks)
    hidden_other = lax.ppermute(hidden_part, "tensor", [(0, 1), (1, 0)])

    return pl.pallas_call(
        functools.partial(output_kernel, slots, rank, half),
        out_shape=jax.ShapeDtypeStruct((rows, out_width), jnp.bfloat16),
        grid_spec=pltpu.PrefetchScalarGridSpec(
            num_scalar_prefetch=2,
            grid=(2,),
            in_specs=[pl.BlockSpec((half, 128), lambda i, m, e: (0, 0))] * 2
            + [pl.BlockSpec((half, out_width), lambda i, m, e: (i, 0))] * 2
            + [pl.BlockSpec((split, ewidth), lambda i, m, e: (0, 0))] * PLANE,
            out_specs=pl.BlockSpec((half, out_width), lambda i, m, e: (i, 0)),
            scratch_shapes=[pltpu.VMEM((split, out_width), jnp.bfloat16)],
        ),
        compiler_params=grant(14),
        cost_estimate=SHORT,
        name="output",
    )(me1, every, hidden_part, hidden_other, base_own, base_other, *blocks)


def solution(mesh):
    replicas = mesh.shape["replica"]
    striped = replicas == 16 and mesh.shape["tensor"] == 2
    return jax.shard_map(
        functools.partial(per_device if striped else per_device_general, replicas=replicas),
        mesh=mesh,
        in_specs=(
            P("replica", "tensor"),
            P("tensor", None),
            P("replica", None, "tensor"),
            P("replica", None, "tensor"),
            P("replica", None),
            P("replica", None),
        ),
        out_specs=P("replica", "tensor"),
        check_vma=False,
    )
```
